32 devices in a mesh: ep: 8 (over z, y), tp: 4 (over x, core).
Axes of the slice: x: 2, y: 2, z: 4, core: 2. Of those that a mesh axis runs over, the one named last changes fastest.
Arguments:
- block_in: bfloat16 [4096, 2048], P('ep'), may hold values from -6 to 6
- input_norm: float32 [2048], replicated, may hold values from 0.25 to 1.75
- q_weight: bfloat16 [2048, 4096], P(None, 'tp'), may hold values from -0.125 to 0.125
- k_weight: bfloat16 [2048, 512], P(None, 'tp'), may hold values from -0.125 to 0.125
- v_weight: bfloat16 [2048, 512], P(None, 'tp'), may hold values from -0.125 to 0.125
- q_gain: float32 [128], replicated, may hold values from 1 to 2
- k_gain: float32 [128], replicated, may hold values from 1 to 1.6
- o_weight: bfloat16 [4096, 2048], P('tp'), may hold values from -0.375 to 0.375
- post_norm: float32 [2048], replicated, may hold values from 0.25 to 1.75
- router: bfloat16 [2048, 32], replicated, may hold values from -0.0625 to 0.0625
- expert_gate: bfloat16 [32, 2048, 768], P('ep', None, 'tp'), may hold values from -0.125 to 0.125
- expert_up: bfloat16 [32, 2048, 768], P('ep', None, 'tp'), may hold values from -0.125 to 0.125
- expert_down: bfloat16 [32, 768, 2048], P('ep', 'tp'), may hold values from -0.875 to 0.875
- expert_ids: int32 [4096, 8], P('ep'), may hold values from 0 to 31, all different within a row; in each aligned block of 512 rows (0 to 511, 512 to 1023, ...) at most 192 rows name the same one
- prefix_len: int32 [2], replicated, may hold values from 204 to 1024
- out_grad: bfloat16 [4096, 2048], P('ep'), may hold values from -6 to 6
Outputs:
- block_out: bfloat16 [4096, 2048], P('ep', 'tp')
- input_grad: bfloat16 [4096, 2048], P('ep')
- input_norm_grad: float32 [2048], replicated
- q_weight_grad: float32 [2048, 4096], P(None, 'tp')
- k_weight_grad: float32 [2048, 512], P(None, 'tp')
- v_weight_grad: float32 [2048, 512], P(None, 'tp')
- q_gain_grad: float32 [128], replicated
- k_gain_grad: float32 [128], replicated
- o_weight_grad: float32 [4096, 2048], P('tp')
- post_norm_grad: float32 [2048], replicated
- router_grad: float32 [2048, 32], replicated
- gate_grad: float32 [32, 2048, 768], P('ep', None, 'tp')
- up_grad: float32 [32, 2048, 768], P('ep', None, 'tp')
- down_grad: float32 [32, 768, 2048], P('ep', 'tp')
The draws below stay inside these ranges and needn't reach their ends.
Inputs may be any that keep to these rules, and one draw needn't show every extreme that they name: `expert_ids`: each token names 8 different experts. Among the 512 tokens of one index of ep no expert is named more than 192 times, and in every draw some expert is named exactly 192 times by the tokens of some index.
All inputs are finite; a program needn't handle non-finite values.
Results may differ from the reference program's by a relative error of at most 0.028.
Values may be sent and summed in bfloat16 or wider, within the bound.
No kernel may reach another device: no remote copies, remote signals or barrier semaphores. Data moves between devices by JAX's collectives and lax.ppermute only.
A program may use at most 512 MiB of HBM per device.

```python
import math
import jax
import jax.numpy as jnp
import numpy as np
from jax import lax

D = 2048
H = 32
KV = 4
HD = 128
FF = 768
TOP = 8
SPAN = 4
TOK_DEV = 512
EXPERTS = 32
SEQ = 2048
SEQS = 2
TOKENS = 4096
CAP = 192
N_EP = 8


def block_scale(own_key, shape, cuts, smallest, largest):
    def one(axis_at, parts):
        heights = jax.random.uniform(jax.random.fold_in(jax.random.fold_in(own_key, 6), axis_at), (parts,), jnp.float32, smallest / len(cuts), largest / len(cuts))
        return jnp.repeat(jnp.exp(heights), shape[axis_at] // parts).reshape((-1,) + (1,) * (len(shape) - axis_at - 1))

    loudness = one(*cuts[0])
    for cut in cuts[1:]:
        loudness = loudness * one(*cut)
    return loudness


def routed_block(stream_key, own, number, rows, amount, top, limit, slope):
    sequence = jax.random.permutation(stream_key, amount)
    packed, usual = shares(amount, rows * top, limit, slope, True), shares(amount, rows * top, limit, slope, False)
    places = jnp.arange(amount)

    def named(lengths, rotation):
        used = int((lengths > 0).sum())
        fixed = max(1, used // 4)
        moved = fixed + (places - fixed + rotation * (used - fixed)) % max(1, amount - fixed)
        return jnp.zeros((amount,), jnp.int32).at[sequence[jnp.where(places < fixed, places, moved)]].set(jnp.asarray(lengths, jnp.int32))

    lengths = jnp.where(number % 4 == 0, named(packed, number // 4), named(usual, number - number // 4 - 1))
    mixed = jax.random.permutation(jax.random.fold_in(own, 3), amount)
    giver, taker = mixed[0:amount // 2 * 2:2], mixed[1:amount // 2 * 2:2]
    room = jnp.minimum(lengths[giver] - 1, limit - lengths[taker]) // 2
    room = jnp.where((giver == sequence[0]) | (taker == sequence[0]) | (lengths[taker] == 0), 0, jnp.maximum(room, 0))
    moved = jax.random.randint(jax.random.fold_in(own, 4), (amount // 2,), 0, 1 << 20) % (room + 1)
    lengths = lengths.at[giver].add(-moved).at[taker].add(moved)
    members = jnp.searchsorted(jnp.cumsum(lengths), jnp.arange(rows * top), side="right").astype(jnp.int32)
    grid = members.reshape(top, rows).T
    grid = grid[jax.random.permutation(jax.random.fold_in(own, 1), rows)]
    rotation = jax.random.randint(jax.random.fold_in(own, 2), (rows, 1), 0, top)
    return jnp.take_along_axis(grid, (jnp.arange(top)[None, :] + rotation) % top, axis=1)


def shares(count, total, bound, slope, full):
    loads = [(1 << 20) // math.isqrt(standing ** slope) + 1 for standing in range(1, count + 1)]
    largest = bound if full else min(bound, max(-(-total // count), total * loads[0] // sum(loads)))
    least = 1 if total - largest >= count - 1 else 0
    given, surplus = [largest] + [least] * (count - 1), total - largest - least * (count - 1)
    while surplus > 0:
        movable = [i for i in range(1, count) if given[i] < largest] or [i for i in range(1, count) if given[i] < bound]
        pool, left = sum([loads[i] for i in movable]), surplus
        for i in movable:
            extra = min(bound - given[i], max(1, left * loads[i] // pool), surplus)
            given[i] = given[i] + extra
            surplus = surplus - extra
    return np.array(given)


def normal_values(rng, extent, deviation, reach, pieces=(), held_as=jnp.bfloat16):
    entries = jax.random.normal(rng, extent, jnp.float32) * deviation
    if len(pieces) > 0:
        entries = block_scale(rng, extent, pieces, -0.22, 0.18) * entries
    return jnp.clip(entries, min=-reach, max=reach).astype(held_as)


def setup_inputs(seed: int = 0) -> dict:
    seeds = jax.random.split(jax.random.key(seed), 17)
    block_in = normal_values(seeds[0], (TOKENS, D), 1.0, 6.0, ((0, 8),))
    input_norm = jnp.clip(1.0 + 0.15 * jax.random.normal(seeds[1], (D,), jnp.float32), 0.25, 1.75)
    q_weight = normal_values(seeds[2], (D, H * HD), D ** -0.5, 0.125, ((1, 4),))
    k_weight = normal_values(seeds[3], (D, KV * HD), D ** -0.5, 0.125, ((1, 4),))
    v_weight = normal_values(seeds[4], (D, KV * HD), D ** -0.5, 0.125, ((1, 4),))
    q_gain = jnp.clip(jax.random.uniform(seeds[5], (HD,), jnp.float32, 1.0, 2.0), 1.0, 2.0)
    k_gain = jnp.clip(jax.random.uniform(seeds[6], (HD,), jnp.float32, 1.0, 1.6), 1.0, 1.6)
    o_weight = normal_values(seeds[7], (H * HD, D), (H * HD // 16) ** -0.5, 0.375, ((0, 4),))
    post_norm = jnp.clip(1.0 + 0.15 * jax.random.normal(seeds[8], (D,), jnp.float32), 0.25, 1.75)
    router = normal_values(seeds[9], (D, EXPERTS), (4 * D) ** -0.5, 0.0625)
    expert_gate = normal_values(seeds[10], (EXPERTS, D, FF), D ** -0.5, 0.125, ((0, 8), (2, 4)))
    expert_up = normal_values(seeds[11], (EXPERTS, D, FF), D ** -0.5, 0.125, ((0, 8), (2, 4)))
    expert_down = normal_values(seeds[12], (EXPERTS, FF, D), (FF // 16) ** -0.5, 0.875, ((0, 8), (1, 4)))
    expert_ids_keys = jax.random.split(jax.random.fold_in(seeds[13], 1), TOKENS // TOK_DEV)
    expert_ids_turns = jax.random.permutation(jax.random.fold_in(seeds[13], 3), TOKENS // TOK_DEV)
    expert_ids = jax.vmap(lambda own, number: routed_block(jax.random.fold_in(seeds[13], 2), own, number, TOK_DEV, EXPERTS, TOP, CAP, 2))(expert_ids_keys, expert_ids_turns).reshape((TOKENS, TOP))
    prefix_len = jax.random.randint(seeds[14], (SEQS,), SEQ // 10, SEQ // 2 + 1).astype(jnp.int32)
    out_grad = normal_values(seeds[15], (TOKENS, D), 1.0, 6.0, ((0, 8),))
    return {"block_in": block_in, "input_norm": input_norm, "q_weight": q_weight, "k_weight": k_weight, "v_weight": v_weight, "q_gain": q_gain, "k_gain": k_gain, "o_weight": o_weight, "post_norm": post_norm, "router": router, "expert_gate": expert_gate, "expert_up": expert_up, "expert_down": expert_down, "expert_ids": expert_ids, "prefix_len": prefix_len, "out_grad": out_grad}


EPSILON = 1e-06
THETA = 1000000.0
MASKED = -1e+30
HIGHEST = lax.Precision.HIGHEST

@jax.custom_vjp
def low(v):
    return lax.optimization_barrier(v.astype(jnp.bfloat16)).astype(jnp.float32)

@jax.custom_vjp
def low_back(v):
    return v

def low_keep(v):
    return (low(v), None)

def low_pass(kept, grad):
    return (grad,)

def back_keep(v):
    return (v, None)

def back_low(kept, grad):
    return (low(grad),)
low.defvjp(low_keep, low_pass)
low_back.defvjp(back_keep, back_low)

def rms_scale(values, scales):
    return values * lax.rsqrt(lax.optimization_barrier(jnp.mean(values * values, axis=-1, keepdims=True)) + EPSILON) * scales

def rotary_tables(positions, head_width):
    half_width = head_width // 2
    exponents = jnp.arange(half_width, dtype=jnp.float32) * (-2.0 / head_width)
    angles = positions.astype(jnp.float32)[:, None] * (THETA ** exponents)[None, :]
    return (jnp.cos(angles), jnp.sin(angles))

def rotate(values, cos_table, sin_table):
    half_width = values.shape[-1] // 2
    shape_rows = (values.shape[0],) + (1,) * (values.ndim - 2) + (half_width,)
    cos_rows = cos_table.reshape(shape_rows)
    sin_rows = sin_table.reshape(shape_rows)
    lead_half = values[..., :half_width]
    tail_half = values[..., half_width:]
    return jnp.concatenate([lead_half * cos_rows - tail_half * sin_rows, tail_half * cos_rows + lead_half * sin_rows], axis=-1)

def matmul(left_part, right_part):
    return jnp.dot(left_part, right_part, precision=HIGHEST)

def seq_positions():
    inner = jnp.arange(SEQ, dtype=jnp.int32)
    return ((inner // TOK_DEV + SPAN - 1) % SPAN * TOK_DEV + inner % TOK_DEV).astype(jnp.int32)

def attend_group(operands):
    query_rows, key_rows, value_rows, prefix = operands
    raw_scores = jnp.einsum('tgd,ud->gtu', query_rows, key_rows, precision=HIGHEST) * HD ** (-0.5)
    scores = low_back(raw_scores)
    places = seq_positions()
    allowed = (places[None, :] <= places[:, None]) | (places[None, :] < prefix)
    probs = jax.nn.softmax(jnp.where(allowed[None], scores, MASKED), axis=-1)
    return jnp.einsum('gtu,ud->tgd', low(probs), value_rows, precision=HIGHEST)

def expert_step(hidden_pad, gate_pad, carry, operands):
    owner_slots, gate_weight, up_weight, down_weight = operands
    row_tokens = owner_slots // TOP
    rows_in = low_back(hidden_pad[row_tokens])
    gate_pre = low_back(matmul(rows_in, gate_weight))
    up_pre = low_back(matmul(rows_in, up_weight))
    hidden_low = low(jax.nn.silu(gate_pre) * up_pre)
    expert_out = low(low_back(matmul(hidden_low, down_weight)))
    weighted = gate_pad[owner_slots][:, None] * expert_out
    return (carry.at[row_tokens].add(weighted), None)

def forward(block_in, input_norm, q_weight, k_weight, v_weight, q_gain, k_gain, o_weight, post_norm, router, expert_gate, expert_up, expert_down, owners, chosen, prefix_rows):
    group_size = H // KV
    attn_low = low(rms_scale(block_in, input_norm))
    q_lin = low_back(matmul(attn_low, q_weight)).reshape(TOKENS, H, HD)
    k_lin = low_back(matmul(attn_low, k_weight)).reshape(TOKENS, KV, HD)
    v_low = low(low_back(matmul(attn_low, v_weight))).reshape(TOKENS, KV, HD)
    positions = jnp.tile(seq_positions(), SEQS)
    cos_table, sin_table = rotary_tables(positions, HD)
    q_low = low(rotate(rms_scale(q_lin, q_gain), cos_table, sin_table))
    k_low = low(rotate(rms_scale(k_lin, k_gain), cos_table, sin_table))
    q_groups = q_low.reshape(SEQS, SEQ, KV, group_size, HD).transpose(0, 2, 1, 3, 4).reshape(SEQS * KV, SEQ, group_size, HD)
    k_groups = k_low.reshape(SEQS, SEQ, KV, HD).transpose(0, 2, 1, 3).reshape(SEQS * KV, SEQ, HD)
    v_groups = v_low.reshape(SEQS, SEQ, KV, HD).transpose(0, 2, 1, 3).reshape(SEQS * KV, SEQ, HD)
    attended = lax.map(jax.checkpoint(attend_group), (q_groups, k_groups, v_groups, prefix_rows))
    o_rows = attended.reshape(SEQS, KV, SEQ, group_size, HD).transpose(0, 2, 1, 3, 4).reshape(TOKENS, H * HD)
    o_low = low(low_back(o_rows))
    x_mid = block_in + low_back(matmul(o_low, o_weight))
    ffn_low = low(rms_scale(x_mid, post_norm))
    logits = low_back(matmul(ffn_low, router))
    picked = lax.optimization_barrier(jnp.sum(jnp.where(chosen, logits[:, None, :], 0.0), axis=-1))
    gate_probs = jax.nn.softmax(picked, axis=-1)
    hidden_pad = jnp.concatenate([ffn_low, jnp.zeros((1, D), jnp.float32)], axis=0)
    gate_pad = jnp.concatenate([gate_probs.reshape(-1), jnp.zeros((1,), jnp.float32)], axis=0)
    step_fn = jax.checkpoint(expert_step)
    mixed, unused = lax.scan(lambda carry, operands: step_fn(hidden_pad, gate_pad, carry, operands), jnp.zeros((TOKENS + 1, D), jnp.float32), (owners, expert_gate, expert_up, expert_down))
    return x_mid + mixed[:TOKENS]

def reference(block_in, input_norm, q_weight, k_weight, v_weight, q_gain, k_gain, o_weight, post_norm, router, expert_gate, expert_up, expert_down, expert_ids, prefix_len, out_grad):
    flat_ids = expert_ids.reshape(-1)
    expert_hits = (flat_ids[:, None] == jnp.arange(EXPERTS, dtype=jnp.int32)[None, :]).astype(jnp.int32)
    slot_ranks = lax.optimization_barrier(jnp.sum(expert_hits * (jnp.cumsum(expert_hits, axis=0) - 1), axis=1)).astype(jnp.int32)
    per_expert = N_EP * CAP
    slot_index = (flat_ids * per_expert + slot_ranks).astype(jnp.int32)
    owners = jnp.full((EXPERTS * per_expert,), TOKENS * TOP, jnp.int32).at[slot_index].set(jnp.arange(TOKENS * TOP, dtype=jnp.int32)).reshape(EXPERTS, per_expert)
    chosen = expert_ids[:, :, None] == jnp.arange(EXPERTS, dtype=jnp.int32)[None, None, :]
    prefix_rows = jnp.repeat(prefix_len, KV)
    floats = [operand.astype(jnp.float32) for operand in (block_in, input_norm, q_weight, k_weight, v_weight, q_gain, k_gain, o_weight, post_norm, router, expert_gate, expert_up, expert_down)]

    def wrapped(*weights):
        return forward(*weights, owners, chosen, prefix_rows)
    result, pull_back = jax.vjp(wrapped, *floats)
    grads = pull_back(out_grad.astype(jnp.float32))
    return (result.astype(jnp.bfloat16), grads[0].astype(jnp.bfloat16), grads[1], grads[2], grads[3], grads[4], grads[5], grads[6], grads[7], grads[8], grads[9], grads[10], grads[11], grads[12])
```

```python
import jax
import jax.numpy as jnp
from jax import lax
from jax.experimental import pallas as pl
from jax.experimental.pallas import tpu as pltpu
from jax.sharding import PartitionSpec as P

SPAN = 4


EPSILON = 1e-06
THETA = 1000000.0
MASKED = -1e30


def shifted(block, axis, distance):
    devices = range(lax.axis_size(axis))
    route = [(i - distance, i) for i in devices if i - distance in devices]
    return lax.ppermute(block, axis, route)


def rms_scale(values, scales):
    return values * lax.rsqrt(jnp.mean(values * values, axis=-1, keepdims=True) + EPSILON) * scales


def rotary_tables(positions, head_width):
    half_width = head_width // 2
    exponents = jnp.arange(half_width, dtype=jnp.float32) * (-2.0 / head_width)
    angles = positions.astype(jnp.float32)[:, None] * (THETA**exponents)[None, :]
    return (jnp.cos(angles), jnp.sin(angles))


def rotate(values, cos_table, sin_table):
    half_width = values.shape[-1] // 2
    shape_rows = (values.shape[0],) + (1,) * (values.ndim - 2) + (half_width,)
    cos_rows = cos_table.reshape(shape_rows)
    sin_rows = sin_table.reshape(shape_rows)
    lead_half = values[..., :half_width]
    tail_half = values[..., half_width:]
    return jnp.concatenate(
        [lead_half * cos_rows - tail_half * sin_rows, tail_half * cos_rows + lead_half * sin_rows],
        axis=-1,
    )


def fetch_rows(pair_rows, distance):
    return shifted((pair_rows[0], pair_rows[1]), "ep", distance)


def return_grads(pair_grads, distance):
    return (
        shifted(pair_grads[0].astype(jnp.bfloat16), "ep", distance).astype(jnp.float32),
        shifted(pair_grads[1].astype(jnp.bfloat16), "ep", distance).astype(jnp.float32),
    )


NT_DIMS = (((1,), (1,)), ((), ()))


def expert_kernel(
    rows_ref,
    cotangent_ref,
    chosen_ref,
    router_ref,
    router_t_ref,
    select_ref,
    gate_ref,
    up_ref,
    down_ref,
    out_ref,
    grad_ref,
    hidden_ref,
    d_gate_ref,
    d_up_ref,
    dlog_ref,
):
    f32 = jnp.float32
    low = jnp.bfloat16
    rows = rows_ref[...]
    logits = jnp.dot(rows, router_ref[...], preferred_element_type=f32)
    logits = jnp.where(chosen_ref[...] > 0.5, logits, MASKED)
    probs = jnp.exp(logits - jnp.max(logits, axis=-1, keepdims=True))
    probs = probs / jnp.sum(probs, axis=-1, keepdims=True)
    select = select_ref[...]
    probs_high = probs.astype(low)
    probs_rest = (probs - probs_high.astype(f32)).astype(low)
    weight = jnp.dot(probs_high, select, preferred_element_type=f32)
    weight += jnp.dot(probs_rest, select, preferred_element_type=f32)
    gate = jnp.dot(rows, gate_ref[...], preferred_element_type=f32)
    up = jnp.dot(rows, up_ref[...], preferred_element_type=f32)
    d_hidden = (
        lax.dot_general(cotangent_ref[...], down_ref[...], NT_DIMS, preferred_element_type=f32)
        * weight
    )
    sig = 1.0 / (1.0 + jnp.exp(-gate))
    silu = gate * sig
    hidden = silu * up
    d_up = (d_hidden * silu).astype(low)
    d_gate = (d_hidden * up * sig * (1.0 + gate * (1.0 - sig))).astype(low)
    hidden_low = (hidden * weight).astype(low)
    dots = lax.dot_general(
        (d_hidden * hidden).astype(low), select, NT_DIMS, preferred_element_type=f32
    )
    dlog = (dots - probs * jnp.sum(dots, axis=-1, keepdims=True)).astype(low)
    hidden_ref[...] = hidden_low
    d_gate_ref[...] = d_gate
    d_up_ref[...] = d_up
    dlog_ref[...] = dlog
    out_ref[...] = jnp.dot(hidden_low, down_ref[...], preferred_element_type=f32).astype(low)
    grads = lax.dot_general(d_gate, gate_ref[...], NT_DIMS, preferred_element_type=f32)
    grads += lax.dot_general(d_up, up_ref[...], NT_DIMS, preferred_element_type=f32)
    grads += jnp.dot(dlog, router_t_ref[...], preferred_element_type=f32)
    grad_ref[...] = grads.astype(low)


def expert_pass(rows, cotangents, chosen, router, select, gate, up, down):
    count, model_width = rows.shape
    experts_all = router.shape[1]
    width = down.shape[0]
    tile = 512

    def tiled(columns):
        return pl.BlockSpec((tile, columns), lambda i: (i, 0))

    def whole(array):
        return pl.BlockSpec(array.shape, lambda i: (0, 0), pipeline_mode=pl.Buffered(1))

    fixed = (router, router.T, select, gate, up, down)
    columns = (model_width, model_width, width, width, width, experts_all)
    return pl.pallas_call(
        expert_kernel,
        grid=(count // tile,),
        in_specs=[tiled(model_width), tiled(model_width), tiled(experts_all)]
        + [whole(array) for array in fixed],
        out_specs=[tiled(size) for size in columns],
        out_shape=[jax.ShapeDtypeStruct((count, size), jnp.bfloat16) for size in columns],
        compiler_params=pltpu.CompilerParams(vmem_limit_bytes=60 * 1024 * 1024),
        cost_estimate=pl.CostEstimate(
            flops=12 * count * model_width * width,
            bytes_accessed=8 * count * model_width,
            transcendentals=count * width,
        ),
    )(rows, cotangents, chosen, *fixed)


def body(
    block_in,
    input_norm,
    q_weight,
    k_weight,
    v_weight,
    q_gain,
    k_gain,
    o_weight,
    post_norm,
    router,
    expert_gate,
    expert_up,
    expert_down,
    expert_ids,
    prefix_len,
    out_grad,
):
    tokens = block_in.shape[0]
    head_width = q_gain.shape[0]
    kv_heads = k_weight.shape[1] // head_width
    group_size = q_weight.shape[1] // head_width // kv_heads
    tp_count = lax.axis_size("tp")
    tp_rank = lax.axis_index("tp")
    ep_count = lax.axis_size("ep")
    ep_rank = lax.axis_index("ep")
    share_rows = tokens // tp_count
    seq_span = SPAN
    dev_slot = ep_rank % seq_span
    block_pos = (dev_slot + seq_span - 1) % seq_span
    prefix = lax.dynamic_index_in_dim(prefix_len, ep_rank // seq_span, keepdims=False)
    row_index = jnp.arange(tokens, dtype=jnp.int32)
    positions = block_pos * tokens + row_index
    score_scale = head_width ** (-0.5)

    def my_rows(full_rows):
        return lax.dynamic_slice_in_dim(full_rows, tp_rank * share_rows, share_rows, 0)

    def sum_rows(partial_rows):
        parts = lax.all_to_all(
            partial_rows.astype(jnp.bfloat16), "tp", split_axis=0, concat_axis=0, tiled=True
        )
        return jnp.sum(
            parts.reshape(tp_count, share_rows, -1).astype(jnp.float32), axis=0
        )

    dy_all = lax.all_gather(my_rows(out_grad), ("ep", "tp"), axis=0, tiled=True)
    x_full = block_in.astype(jnp.float32)
    attn_low = rms_scale(x_full, input_norm).astype(jnp.bfloat16)
    q_lin = jnp.dot(attn_low, q_weight, preferred_element_type=jnp.float32).reshape(
        tokens, kv_heads, group_size, head_width
    )
    k_lin = jnp.dot(attn_low, k_weight, preferred_element_type=jnp.float32).reshape(
        tokens, kv_heads, head_width
    )
    v_lin = jnp.dot(attn_low, v_weight, preferred_element_type=jnp.float32).reshape(
        tokens, kv_heads, head_width
    )
    cos_table, sin_table = rotary_tables(positions, head_width)

    def head_path(lin_rows, scales):
        return rotate(rms_scale(lin_rows, scales), cos_table, sin_table)

    q_rot, q_back = jax.vjp(head_path, q_lin, q_gain)
    k_rot, k_back = jax.vjp(head_path, k_lin, k_gain)
    q_low = q_rot.astype(jnp.bfloat16)
    k_low = k_rot.astype(jnp.bfloat16)
    v_low = v_lin.astype(jnp.bfloat16)
    distances = list(range(seq_span))
    key_blocks = []
    allowed_blocks = []
    for distance in distances:
        if distance == 0:
            pair_rows = (k_low, v_low)
        else:
            below = fetch_rows((k_low, v_low), distance)
            above = fetch_rows((k_low, v_low), distance - seq_span)
            use_below = dev_slot >= distance
            pair_rows = (
                jnp.where(use_below, below[0], above[0]),
                jnp.where(use_below, below[1], above[1]),
            )
        source_slot = (dev_slot - distance) % seq_span
        source_pos = (source_slot + seq_span - 1) % seq_span
        key_pos = source_pos * tokens + row_index
        allowed = (key_pos[None, :] <= positions[:, None]) | (key_pos[None, :] < prefix)
        key_blocks.append(pair_rows)
        allowed_blocks.append(allowed)

    def block_scores(pair_rows, allowed):
        raw_scores = (
            jnp.einsum("tkgd,ukd->kgtu", q_low, pair_rows[0], preferred_element_type=jnp.float32)
            * score_scale
        )
        return jnp.where(allowed[None, None], raw_scores, MASKED)

    def block_probs(pair_rows, allowed, log_total):
        return jnp.where(
            allowed[None, None],
            jnp.exp(block_scores(pair_rows, allowed) - log_total[..., None]),
            0.0,
        )

    log_total = jnp.full((kv_heads, group_size, tokens), MASKED, jnp.float32)
    for pair_rows, allowed in zip(key_blocks, allowed_blocks):
        log_total = jnp.logaddexp(
            log_total, jax.nn.logsumexp(block_scores(pair_rows, allowed), axis=-1)
        )
    attn_acc = jnp.zeros((tokens, kv_heads, group_size, head_width), jnp.float32)
    for pair_rows, allowed in zip(key_blocks, allowed_blocks):
        prob_low = block_probs(pair_rows, allowed, log_total).astype(jnp.bfloat16)
        attn_acc = attn_acc + jnp.einsum(
            "kgtu,ukd->tkgd", prob_low, pair_rows[1], preferred_element_type=jnp.float32
        )
    o_low = attn_acc.reshape(tokens, -1).astype(jnp.bfloat16)
    head_part = jnp.dot(o_low, o_weight, preferred_element_type=jnp.float32)
    x_mid = my_rows(x_full) + sum_rows(head_part)
    ffn_in, post_norm_back = jax.vjp(rms_scale, x_mid, post_norm)
    ffn_all = lax.all_gather(ffn_in.astype(jnp.bfloat16), ("ep", "tp"), axis=0, tiled=True)
    experts_all = router.shape[1]
    local_experts = expert_gate.shape[0]
    hidden_width = expert_gate.shape[2]
    ids_all = lax.all_gather(expert_ids, "ep", axis=0, tiled=True)
    expert_index = jnp.arange(experts_all, dtype=jnp.int32)
    chosen = jnp.any(ids_all[:, :, None] == expert_index[None, None, :], axis=1)
    chosen_low = chosen.astype(jnp.bfloat16)
    width = local_experts * hidden_width
    own_expert = ep_rank * local_experts + jnp.arange(width, dtype=jnp.int32) // hidden_width
    select = (expert_index[:, None] == own_expert[None, :]).astype(jnp.bfloat16)
    gate_cat = expert_gate.transpose(1, 0, 2).reshape(-1, width)
    up_cat = expert_up.transpose(1, 0, 2).reshape(-1, width)
    down_cat = expert_down.reshape(width, -1)
    expert_out, row_grads, hidden_low, d_gate_low, d_up_low, dlog_low = expert_pass(
        ffn_all, dy_all, chosen_low, router, select, gate_cat, up_cat, down_cat
    )
    d_ffn = lax.psum_scatter(
        row_grads, ("ep", "tp"), scatter_dimension=0, tiled=True
    ).astype(jnp.float32)
    mixed = lax.psum_scatter(
        expert_out, ("ep", "tp"), scatter_dimension=0, tiled=True
    ).astype(jnp.float32)
    block_rows = (x_mid + mixed).astype(jnp.bfloat16)
    block_out = lax.all_to_all(block_rows, "tp", split_axis=1, concat_axis=0, tiled=True)
    down_grad = jnp.einsum(
        "tf,td->fd", hidden_low, dy_all, preferred_element_type=jnp.float32
    ).reshape(expert_down.shape)
    gate_grad = jnp.einsum("td,tf->df", ffn_all, d_gate_low, preferred_element_type=jnp.float32)
    up_grad = jnp.einsum("td,tf->df", ffn_all, d_up_low, preferred_element_type=jnp.float32)
    gate_grad = gate_grad.reshape(-1, local_experts, hidden_width).transpose(1, 0, 2)
    up_grad = up_grad.reshape(-1, local_experts, hidden_width).transpose(1, 0, 2)
    router_grad = jnp.einsum("td,te->de", ffn_all, dlog_low, preferred_element_type=jnp.float32)
    d_mid_norm, post_norm_grad = post_norm_back(d_ffn)
    d_mid = my_rows(out_grad).astype(jnp.float32) + d_mid_norm
    d_mid_low = lax.all_gather(d_mid.astype(jnp.bfloat16), "tp", axis=0, tiled=True)
    o_weight_grad = jnp.einsum("tj,td->jd", o_low, d_mid_low, preferred_element_type=jnp.float32)
    d_attn_low = (
        jnp.einsum("td,jd->tj", d_mid_low, o_weight, preferred_element_type=jnp.float32)
        .astype(jnp.bfloat16)
        .reshape(tokens, kv_heads, group_size, head_width)
    )
    row_delta = jnp.sum(d_attn_low.astype(jnp.float32) * attn_acc, axis=-1).transpose(1, 2, 0)
    q_grad_rot = jnp.zeros((tokens, kv_heads, group_size, head_width), jnp.float32)
    k_grad_rot = jnp.zeros((tokens, kv_heads, head_width), jnp.float32)
    v_grad_sum = jnp.zeros((tokens, kv_heads, head_width), jnp.float32)
    for distance, pair_rows, allowed in zip(distances, key_blocks, allowed_blocks):
        probs = block_probs(pair_rows, allowed, log_total)
        d_probs = jnp.einsum(
            "tkgd,ukd->kgtu", d_attn_low, pair_rows[1], preferred_element_type=jnp.float32
        )
        d_scores = (probs * (d_probs - row_delta[..., None])).astype(jnp.bfloat16)
        q_grad_rot = (
            q_grad_rot
            + jnp.einsum(
                "kgtu,ukd->tkgd", d_scores, pair_rows[0], preferred_element_type=jnp.float32
            )
            * score_scale
        )
        key_grad = (
            jnp.einsum("kgtu,tkgd->ukd", d_scores, q_low, preferred_element_type=jnp.float32)
            * score_scale
        )
        value_grad = jnp.einsum(
            "kgtu,tkgd->ukd",
            probs.astype(jnp.bfloat16),
            d_attn_low,
            preferred_element_type=jnp.float32,
        )
        if distance == 0:
            k_grad_rot = key_grad
            v_grad_sum = value_grad
        else:
            use_below = dev_slot >= distance
            back_below = return_grads(
                (jnp.where(use_below, key_grad, 0.0), jnp.where(use_below, value_grad, 0.0)),
                -distance,
            )
            back_above = return_grads(
                (jnp.where(use_below, 0.0, key_grad), jnp.where(use_below, 0.0, value_grad)),
                seq_span - distance,
            )
            k_grad_rot = k_grad_rot + back_below[0] + back_above[0]
            v_grad_sum = v_grad_sum + back_below[1] + back_above[1]
    dq_lin, q_gain_grad = q_back(q_grad_rot)
    dk_lin, k_gain_grad = k_back(k_grad_rot)
    dq_low = dq_lin.reshape(tokens, -1).astype(jnp.bfloat16)
    dk_low = dk_lin.reshape(tokens, -1).astype(jnp.bfloat16)
    dv_low = v_grad_sum.reshape(tokens, -1).astype(jnp.bfloat16)
    q_weight_grad = jnp.einsum("td,tj->dj", attn_low, dq_low, preferred_element_type=jnp.float32)
    k_weight_grad = jnp.einsum("td,tj->dj", attn_low, dk_low, preferred_element_type=jnp.float32)
    v_weight_grad = jnp.einsum("td,tj->dj", attn_low, dv_low, preferred_element_type=jnp.float32)
    d_attn_in = jnp.einsum("tj,dj->td", dq_low, q_weight, preferred_element_type=jnp.float32)
    d_attn_in = d_attn_in + jnp.einsum(
        "tj,dj->td", dk_low, k_weight, preferred_element_type=jnp.float32
    )
    d_attn_in = d_attn_in + jnp.einsum(
        "tj,dj->td", dv_low, v_weight, preferred_element_type=jnp.float32
    )
    d_attn_rows = sum_rows(d_attn_in)
    x_rows = my_rows(x_full)
    _, input_norm_rows = jax.vjp(rms_scale, x_rows, input_norm)
    d_in_norm, input_norm_grad = input_norm_rows(d_attn_rows)
    input_grad = lax.all_gather(
        (d_mid + d_in_norm).astype(jnp.bfloat16), "tp", axis=0, tiled=True
    )
    (q_weight_grad, k_weight_grad, v_weight_grad, o_weight_grad) = (
        lax.psum(q_weight_grad.astype(jnp.bfloat16), "ep").astype(jnp.float32),
        lax.psum(k_weight_grad.astype(jnp.bfloat16), "ep").astype(jnp.float32),
        lax.psum(v_weight_grad.astype(jnp.bfloat16), "ep").astype(jnp.float32),
        lax.psum(o_weight_grad.astype(jnp.bfloat16), "ep").astype(jnp.float32),
    )
    (router_grad, input_norm_grad, post_norm_grad, q_gain_grad, k_gain_grad) = lax.psum(
        (router_grad, input_norm_grad, post_norm_grad, q_gain_grad, k_gain_grad), ("ep", "tp")
    )
    return (
        block_out,
        input_grad,
        input_norm_grad,
        q_weight_grad,
        k_weight_grad,
        v_weight_grad,
        q_gain_grad,
        k_gain_grad,
        o_weight_grad,
        post_norm_grad,
        router_grad,
        gate_grad,
        up_grad,
        down_grad,
    )


def solution(mesh):
    in_specs = (
        P("ep", None),
        P(),
        P(None, "tp"),
        P(None, "tp"),
        P(None, "tp"),
        P(),
        P(),
        P("tp", None),
        P(),
        P(),
        P("ep", None, "tp"),
        P("ep", None, "tp"),
        P("ep", "tp", None),
        P("ep", None),
        P(),
        P("ep", None),
    )
    out_specs = (
        P("ep", "tp"),
        P("ep", None),
        P(),
        P(None, "tp"),
        P(None, "tp"),
        P(None, "tp"),
        P(),
        P(),
        P("tp", None),
        P(),
        P(),
        P("ep", None, "tp"),
        P("ep", None, "tp"),
        P("ep", "tp", None),
    )
    return jax.shard_map(body, mesh=mesh, in_specs=in_specs, out_specs=out_specs, check_vma=False)
```

```python
import jax
import jax.numpy as jnp
from jax import lax
from jax.experimental import pallas as pl
from jax.experimental.pallas import tpu as pltpu
from jax.sharding import PartitionSpec as P

SPAN = 4
EPSILON = 1e-06
THETA = 1000000.0
MASKED = -1e30
LOG2E = 1.4426950408889634
NT_DIMS = (((1,), (1,)), ((), ()))
TN_DIMS = (((0,), (0,)), ((), ()))
VMEM_LIMIT = 60 * 1024 * 1024
TILE = 256
CHUNKS = 4
F32 = jnp.float32
LOW = jnp.bfloat16


def rms_scale(values, scales):
    return values * lax.rsqrt(jnp.mean(values * values, axis=-1, keepdims=True) + EPSILON) * scales


def swap(block, axis, mask):
    devices = range(lax.axis_size(axis))
    return lax.ppermute(block, axis, [(i, i ^ mask) for i in devices])


def turn(block, step):
    count = lax.axis_size("ep")
    return lax.ppermute(block, "ep", [(i, (i + 2 * step) % count) for i in range(count)])


def add_low(kept, received):
    return (kept.astype(F32) + received.astype(F32)).astype(LOW)


def tie(*values):
    return lax.optimization_barrier(values)


def paired(block, axis, mask):
    return jnp.concatenate([block, swap(block, axis, mask)], axis=0)


def spread_start(slots):
    half = slots[0].shape[0] // 2
    first = jnp.concatenate([rows[:half] for rows in slots], axis=0)
    second = jnp.concatenate([rows[half:] for rows in slots], axis=0)
    return paired(first, "tp", 2), paired(second, "ep", 1)


def spread_next(first, second):
    return jnp.concatenate([paired(first, "ep", 1), paired(second, "tp", 2)], axis=0)


def halves(block):
    size = block.shape[0] // 2
    return block[:size], block[size:]


def fold(block, axis, mask):
    kept, sent = halves(block)
    return add_low(kept, swap(sent, axis, mask))


def fold_inner(block, axis, mask):
    parts = block.reshape(2, 2, -1, block.shape[1])
    kept = add_low(parts[:, 0], swap(parts[:, 1], axis, mask))
    return kept.reshape(-1, block.shape[1])


def collect_start(kept, sent):
    return halves(add_low(kept, swap(sent, "tp", 1)))


def collect_next(first, second):
    return fold(first, "ep", 1), fold(second, "tp", 2)


def collect_last(first, second):
    return fold(first, "tp", 2), fold(second, "ep", 1)


def slot_rows(first, second, count):
    parts = [part.reshape(count, -1, part.shape[1]) for part in (first, second)]
    return jnp.concatenate(parts, axis=1)


def pick(array, index, axis=0):
    return lax.dynamic_index_in_dim(array, index, axis, keepdims=False)


def ep_masks():
    return [1 << n for n in range(lax.axis_size("ep").bit_length() - 1)]


def halve_sum(block, mask):
    bit = lax.axis_index("ep") // mask % 2
    parts = block.reshape(2, -1, block.shape[1])
    return add_low(pick(parts, bit), swap(pick(parts, 1 - bit), "ep", mask))


def double(block, mask):
    bit = lax.axis_index("ep") // mask % 2
    other = swap(block, "ep", mask)
    low = jnp.where(bit == 0, block, other)
    high = jnp.where(bit == 0, other, block)
    return jnp.concatenate([low, high], axis=0)


def sum_all(values):
    for axis in ("tp", "ep"):
        mask = 1
        while mask < lax.axis_size(axis):
            values = values + swap(values, axis, mask)
            mask *= 2
    return values


def expert_kernel(
    own_ref,
    other_ref,
    cotangent_own_ref,
    cotangent_other_ref,
    router_ref,
    router_t_ref,
    select_ref,
    gate_ref,
    up_ref,
    down_ref,
    *refs,
):
    grad_keep_ref, grad_send_ref, out_keep_ref, out_send_ref = refs[-10:-6]
    rows_ref, cotangents_ref, hidden_ref, d_gate_ref, d_up_ref, dlog_ref = refs[-6:]
    is_own = pl.program_id(0) < pl.num_programs(0) // 2
    rows = jnp.where(is_own, own_ref[...], other_ref[...])
    model_width = rows.shape[1]
    cotangents = jnp.where(is_own, cotangent_own_ref[...], cotangent_other_ref[...])
    cotangents = cotangents.reshape(rows.shape[0], -1)
    chosen = cotangents[:, model_width : model_width + router_ref.shape[1]].astype(F32)
    logits = jnp.dot(rows, router_ref[...], preferred_element_type=F32)
    logits = jnp.where(chosen > 0.5, logits, MASKED)
    probs = jnp.exp(logits - jnp.max(logits, axis=-1, keepdims=True))
    probs = probs / jnp.sum(probs, axis=-1, keepdims=True)
    select = select_ref[...]
    probs_high = probs.astype(LOW)
    probs_rest = (probs - probs_high.astype(F32)).astype(LOW)
    weight = jnp.dot(probs_high, select, preferred_element_type=F32)
    weight += jnp.dot(probs_rest, select, preferred_element_type=F32)
    gate = jnp.dot(rows, gate_ref[...], preferred_element_type=F32)
    up = jnp.dot(rows, up_ref[...], preferred_element_type=F32)
    d_hidden = (
        lax.dot_general(
            cotangents[:, :model_width], down_ref[...], NT_DIMS, preferred_element_type=F32
        )
        * weight
    )
    sig = 1.0 / (1.0 + jnp.exp(-gate))
    silu = gate * sig
    hidden = silu * up
    d_up = (d_hidden * silu).astype(LOW)
    d_gate = (d_hidden * up * sig * (1.0 + gate * (1.0 - sig))).astype(LOW)
    hidden_low = (hidden * weight).astype(LOW)
    dots = lax.dot_general(
        (d_hidden * hidden).astype(LOW), select, NT_DIMS, preferred_element_type=F32
    )
    dlog = (dots - probs * jnp.sum(dots, axis=-1, keepdims=True)).astype(LOW)

    def store(ref, values):
        ref[...] = values.reshape(ref.shape)

    def store_either(keep_ref, send_ref, values):
        @pl.when(is_own)
        def _():
            store(keep_ref, values)

        @pl.when(jnp.logical_not(is_own))
        def _():
            store(send_ref, values)

    store(rows_ref, rows)
    store(cotangents_ref, cotangents[:, :model_width])
    store(hidden_ref, hidden_low)
    store(d_gate_ref, d_gate)
    store(d_up_ref, d_up)
    store(dlog_ref, dlog)
    outs = jnp.dot(hidden_low, down_ref[...], preferred_element_type=F32).astype(LOW)
    store_either(out_keep_ref, out_send_ref, outs)
    grads = lax.dot_general(d_gate, gate_ref[...], NT_DIMS, preferred_element_type=F32)
    grads += lax.dot_general(d_up, up_ref[...], NT_DIMS, preferred_element_type=F32)
    grads += jnp.dot(dlog, router_t_ref[...], preferred_element_type=F32)
    store_either(grad_keep_ref, grad_send_ref, grads.astype(LOW))


def expert_pass(own, other, cotangents, at, chunk, slots_all, fixed, kept):
    count, model_width = own.shape
    groups, _, unit, wide = cotangents[0].shape
    slots = slots_all // CHUNKS
    half = count // TILE
    width = fixed[-1].shape[0]
    experts_all = fixed[0].shape[1]
    block = TILE // (slots * unit)

    def first(i):
        return jnp.minimum(i, half - 1)

    def second(i):
        return jnp.maximum(i - half, 0)

    def every(i):
        return i

    def rows_spec(index):
        return pl.BlockSpec((TILE, model_width), lambda i: (index(i), 0))

    def placed(columns, index, where):
        return pl.BlockSpec((block, slots, unit, columns), lambda i: (index(i), where, 0, 0))

    def whole(array):
        return pl.BlockSpec(array.shape, lambda i: (0, 0), pipeline_mode=pl.Buffered(1))

    columns = (model_width, model_width, width, width, width, experts_all)
    in_specs = [
        rows_spec(first),
        rows_spec(second),
        placed(wide, first, at),
        placed(wide, second, at),
    ] + [whole(array) for array in fixed]
    aliases = {len(in_specs) + n: 2 + n for n in range(len(kept))}
    part = jax.ShapeDtypeStruct((count, model_width), LOW)
    place = jax.ShapeDtypeStruct((groups, slots_all, unit, model_width), LOW)
    return pl.pallas_call(
        expert_kernel,
        grid=(2 * half,),
        in_specs=in_specs + [pl.BlockSpec(memory_space=pl.ANY)] * len(kept),
        out_specs=[
            rows_spec(first),
            rows_spec(second),
            placed(model_width, first, chunk),
            placed(model_width, second, chunk),
        ]
        + [placed(size, every, chunk) for size in columns],
        out_shape=[part, part, place, place]
        + [jax.ShapeDtypeStruct((2 * groups, slots_all, unit, size), LOW) for size in columns],
        input_output_aliases=aliases,
        compiler_params=pltpu.CompilerParams(vmem_limit_bytes=VMEM_LIMIT),
        cost_estimate=pl.CostEstimate(
            flops=24 * count * model_width * width,
            bytes_accessed=20 * count * model_width,
            transcendentals=2 * count * width,
        ),
        name="expert_pass",
    )(own, other, *cotangents, *fixed, *kept)


def turned_halves(values):
    return pltpu.roll(values, values.shape[1] // 2, 1)


def head_rows(lin, gain, cos, sin):
    scale = lax.rsqrt(jnp.mean(lin * lin, axis=-1, keepdims=True) + EPSILON)
    hat = lin * scale
    normed = hat * gain
    return scale, hat, normed * cos + turned_halves(normed) * sin


def allowed_keys(place_ref, block, keys, queries):
    key_pos = place_ref[2 + block] + lax.broadcasted_iota(jnp.int32, (keys, 1), 0)
    key_pos = jnp.where(key_pos < place_ref[1], -1, key_pos)
    query_pos = place_ref[0] + lax.broadcasted_iota(jnp.int32, (1, queries), 1)
    return key_pos <= query_pos


def attend_kernel(
    place_ref, q_ref, gain_ref, cos_ref, sin_ref, k_ref, v_t_ref, o_ref, norm_ref
):
    queries, head_width = q_ref.shape
    _, _, q_rot = head_rows(q_ref[...], gain_ref[...], cos_ref[...], sin_ref[...])
    q_low = q_rot.astype(LOW)
    factor = head_width ** (-0.5) * LOG2E
    total = jnp.zeros((1, queries), F32)
    acc = jnp.zeros((head_width, queries), F32)
    for block in range(SPAN):
        span = pl.ds(block * queries, queries)
        scores = lax.dot_general(k_ref[span, :], q_low, NT_DIMS, preferred_element_type=F32)
        probs = jnp.where(
            allowed_keys(place_ref, block, queries, queries), jnp.exp2(scores * factor), 0.0
        )
        total += jnp.sum(probs, axis=0, keepdims=True)
        acc += jnp.dot(v_t_ref[:, span], probs.astype(LOW), preferred_element_type=F32)
    o_ref[...] = (acc / total).T.astype(LOW)
    norm_ref[0] = 1.0 / total


def attend(place, q_lin, gain, cos, sin, k_all, v_t):
    tokens, columns = q_lin.shape
    head_width = gain.shape[1]
    heads = columns // head_width
    row = pl.BlockSpec((tokens, head_width), lambda h, p: (0, h))

    def whole(array):
        return pl.BlockSpec(array.shape, lambda h, p: (0, 0))

    return pl.pallas_call(
        attend_kernel,
        grid_spec=pltpu.PrefetchScalarGridSpec(
            num_scalar_prefetch=1,
            grid=(heads,),
            in_specs=[row] + [whole(x) for x in (gain, cos, sin, k_all, v_t)],
            out_specs=[row, pl.BlockSpec((1, 1, tokens), lambda h, p: (h, 0, 0))],
        ),
        out_shape=[
            jax.ShapeDtypeStruct((tokens, columns), LOW),
            jax.ShapeDtypeStruct((heads, 1, tokens), F32),
        ],
        compiler_params=pltpu.CompilerParams(vmem_limit_bytes=VMEM_LIMIT),
        cost_estimate=pl.CostEstimate(
            flops=16 * SPAN * tokens * tokens * columns // 8 * 2,
            bytes_accessed=8 * tokens * columns,
            transcendentals=SPAN * tokens * tokens * heads,
        ),
        name="attend",
    )(place, q_lin, gain, cos, sin, k_all, v_t)


def attend_back_kernel(
    place_ref,
    q_ref,
    d_ref,
    gain_ref,
    cos_ref,
    sin_ref,
    k_ref,
    k_t_ref,
    v_ref,
    norm_ref,
    dq_ref,
    dk_ref,
    dv_ref,
    dgain_ref,
):
    queries, head_width = q_ref.shape
    gain = gain_ref[...]
    scale, hat, q_rot = head_rows(q_ref[...], gain, cos_ref[...], sin_ref[...])
    q_low = q_rot.astype(LOW)
    d_low = d_ref[...]
    shrink = head_width ** (-0.5)
    factor = shrink * LOG2E
    inverse = norm_ref[0]
    delta = jnp.zeros((1, queries), F32)
    kept = []

    @pl.when(pl.program_id(0) == 0)
    def _():
        dk_ref[...] = jnp.zeros_like(dk_ref)
        dv_ref[...] = jnp.zeros_like(dv_ref)
        dgain_ref[...] = jnp.zeros_like(dgain_ref)

    for block in range(SPAN):
        span = pl.ds(block * queries, queries)
        scores = lax.dot_general(k_ref[span, :], q_low, NT_DIMS, preferred_element_type=F32)
        probs = jnp.where(
            allowed_keys(place_ref, block, queries, queries),
            jnp.exp2(scores * factor) * inverse,
            0.0,
        )
        d_probs = lax.dot_general(v_ref[span, :], d_low, NT_DIMS, preferred_element_type=F32)
        delta += jnp.sum(probs * d_probs, axis=0, keepdims=True)
        dv_ref[span, :] += jnp.dot(probs.astype(LOW), d_low, preferred_element_type=F32)
        kept.append((probs, d_probs))
    acc = jnp.zeros((head_width, queries), F32)
    for block in range(SPAN):
        span = pl.ds(block * queries, queries)
        probs, d_probs = kept[block]
        d_scores = (probs * (d_probs - delta)).astype(LOW)
        dk_ref[span, :] += jnp.dot(d_scores, q_low, preferred_element_type=F32) * shrink
        acc += jnp.dot(k_t_ref[:, span], d_scores, preferred_element_type=F32)
    d_rot = acc.T * shrink
    d_normed = d_rot * cos_ref[...] + turned_halves(d_rot * sin_ref[...])
    dgain_ref[...] += jnp.sum(d_normed * hat, axis=0, keepdims=True)
    scaled = d_normed * gain
    d_lin = scale * (scaled - hat * jnp.mean(scaled * hat, axis=-1, keepdims=True))
    dq_ref[...] = d_lin.astype(LOW)


def attend_back(place, q_lin, d_attn, gain, cos, sin, k_all, v_all, inverse):
    tokens, columns = q_lin.shape
    head_width = gain.shape[1]
    heads = columns // head_width
    keys = k_all.shape[0]
    row = pl.BlockSpec((tokens, head_width), lambda h, p: (0, h))
    k_t = k_all.T

    def whole(shape):
        return pl.BlockSpec(shape, lambda h, p: (0, 0))

    fixed = (gain, cos, sin, k_all, k_t, v_all)
    return pl.pallas_call(
        attend_back_kernel,
        grid_spec=pltpu.PrefetchScalarGridSpec(
            num_scalar_prefetch=1,
            grid=(heads,),
            in_specs=[row, row]
            + [whole(x.shape) for x in fixed]
            + [pl.BlockSpec((1, 1, tokens), lambda h, p: (h, 0, 0))],
            out_specs=[
                row,
                whole((keys, head_width)),
                whole((keys, head_width)),
                whole((1, head_width)),
            ],
        ),
        out_shape=[
            jax.ShapeDtypeStruct((tokens, columns), LOW),
            jax.ShapeDtypeStruct((keys, head_width), F32),
            jax.ShapeDtypeStruct((keys, head_width), F32),
            jax.ShapeDtypeStruct((1, head_width), F32),
        ],
        compiler_params=pltpu.CompilerParams(vmem_limit_bytes=VMEM_LIMIT),
        cost_estimate=pl.CostEstimate(
            flops=20 * keys * tokens * columns,
            bytes_accessed=8 * tokens * columns,
            transcendentals=keys * tokens * heads,
        ),
        name="attend_back",
    )(place, q_lin, d_attn, *fixed, inverse)


def body(
    block_in,
    input_norm,
    q_weight,
    k_weight,
    v_weight,
    q_gain,
    k_gain,
    o_weight,
    post_norm,
    router,
    expert_gate,
    expert_up,
    expert_down,
    expert_ids,
    prefix_len,
    out_grad,
):
    tokens, model_width = block_in.shape
    head_width = q_gain.shape[0]
    tp_count = lax.axis_size("tp")
    tp_rank = lax.axis_index("tp")
    ep_count = lax.axis_size("ep")
    ep_rank = lax.axis_index("ep")
    share_rows = tokens // tp_count
    dev_slot = ep_rank % SPAN
    prefix = lax.dynamic_index_in_dim(prefix_len, ep_rank // SPAN, keepdims=False)
    core_bit = tp_rank % 2
    x_bit = tp_rank // 2
    row_index = jnp.arange(tokens, dtype=jnp.int32)
    slots_all = ep_count // 2

    def block_place(slot):
        return (slot + SPAN - 1) % SPAN * tokens

    def my_rows(full_rows):
        return lax.dynamic_slice_in_dim(full_rows, tp_rank * share_rows, share_rows, 0)

    def sum_rows(partial_rows):
        parts = partial_rows.reshape(2, 2, share_rows, -1)

        sent = swap(pick(parts, 1 - core_bit, 1).astype(LOW), "tp", 1)
        parts = pick(parts, core_bit, 1) + sent.astype(F32)
        sent = swap(pick(parts, 1 - x_bit, 0).astype(LOW), "tp", 2)
        return pick(parts, x_bit, 0) + sent.astype(F32)

    def join_rows(rows):
        other = swap(rows, "tp", 2)
        pair = jnp.stack([jnp.where(x_bit == 0, rows, other), jnp.where(x_bit == 0, other, rows)])
        other = swap(pair, "tp", 1)
        low = jnp.where(core_bit == 0, pair, other)
        high = jnp.where(core_bit == 0, other, pair)
        return jnp.stack([low, high], axis=1).reshape(tokens, -1)

    experts_all = router.shape[1]
    local_experts = expert_gate.shape[0]
    hidden_width = expert_gate.shape[2]
    expert_index = jnp.arange(experts_all, dtype=jnp.int32)
    width = local_experts * hidden_width

    chosen = jnp.any(my_rows(expert_ids)[:, :, None] == expert_index[None, None, :], axis=1)
    chosen = jnp.pad(chosen.astype(LOW), ((0, 0), (0, -experts_all % 128)))
    wide_rows = jnp.concatenate([my_rows(out_grad), chosen], axis=1)
    per_chunk = slots_all // CHUNKS
    order = [c * per_chunk + at for c in (0, 1, 3, 2) for at in range(per_chunk)]
    unit = share_rows // 2

    def fetch(rows, positions):
        return [
            rows if order[p] == 0 else turn(rows, slots_all - order[p])
            for c in positions
            for p in range(c * per_chunk, (c + 1) * per_chunk)
        ]

    wide_first = spread_start(fetch(wide_rows, (0,)))
    large = slots_all > CHUNKS
    near_groups = ((1,), (2,)) if large else ((1, 2),)
    wide_near = [fetch(wide_rows, group) for group in near_groups]

    x_full = block_in.astype(F32)
    attn_low = rms_scale(x_full, input_norm).astype(LOW)
    k_lin = jnp.dot(attn_low, k_weight, preferred_element_type=F32)
    v_low = jnp.dot(attn_low, v_weight, preferred_element_type=F32).astype(LOW)
    half_width = head_width // 2
    exponents = jnp.arange(half_width, dtype=F32) * (-2.0 / head_width)
    positions = block_place(dev_slot) + row_index
    angles = positions.astype(F32)[:, None] * (THETA**exponents)[None, :]
    cos_half, sin_half = jnp.cos(angles), jnp.sin(angles)
    cos = jnp.concatenate([cos_half, cos_half], axis=1)
    sin = jnp.concatenate([-sin_half, sin_half], axis=1)

    def key_path(lin_rows, scales):
        normed = rms_scale(lin_rows, scales)
        lead, tail = normed[:, :half_width], normed[:, half_width:]
        return normed * cos + jnp.concatenate([tail, lead], axis=1) * sin

    k_rot, k_back = jax.vjp(key_path, k_lin, k_gain)
    pair = jnp.concatenate([k_rot.astype(LOW), v_low], axis=1)
    pair, *wide_first = tie(pair, *wide_first)
    pairs = [pair] + [swap(pair, "ep", d) for d in range(1, SPAN)]
    wide_first = spread_next(*wide_first)
    q_lin = jnp.dot(attn_low, q_weight, preferred_element_type=F32)
    width_own = local_experts * hidden_width
    gate_cat = expert_gate.transpose(1, 0, 2).reshape(-1, width_own)
    up_cat = expert_up.transpose(1, 0, 2).reshape(-1, width_own)
    gate_cat, up_cat, q_lin, wide_first, wide_rows, pairs, wide_near = tie(
        gate_cat, up_cat, q_lin, wide_first, wide_rows, pairs, wide_near
    )
    wide_far = fetch(wide_rows, (3,))
    wide_near = [spread_start(group) for group in wide_near]
    wide_first_other = swap(wide_first, "tp", 1)
    k_all = jnp.concatenate([p[:, :head_width] for p in pairs], axis=0)
    v_all = jnp.concatenate([p[:, head_width:] for p in pairs], axis=0)
    place = jnp.stack(
        [block_place(dev_slot), prefix] + [block_place(dev_slot ^ d) for d in range(SPAN)]
    ).astype(jnp.int32)
    gain_row = q_gain.reshape(1, -1)
    o_low, inverse = attend(place, q_lin, gain_row, cos, sin, k_all, v_all.T)
    o_low, wide_first_other, wide_near = tie(o_low, wide_first_other, wide_near)
    wide_near = [spread_next(*group) for group in wide_near]
    head_part = jnp.dot(o_low, o_weight, preferred_element_type=F32)
    x_mid = my_rows(x_full) + sum_rows(head_part)
    ffn_in, post_norm_back = jax.vjp(rms_scale, x_mid, post_norm)
    ffn_low = ffn_in.astype(LOW)
    ffn_low, *wide_far = tie(ffn_low, *wide_far)

    own_expert = ep_rank * local_experts + jnp.arange(width, dtype=jnp.int32) // hidden_width
    select = (expert_index[:, None] == own_expert[None, :]).astype(LOW)
    down_cat = expert_down.reshape(width, -1)
    fixed = (router, router.T, select, gate_cat, up_cat, down_cat)
    started = {c: spread_start(fetch(ffn_low, (c,))) for c in range(3)}
    owned = {c: spread_next(*started[c]) for c in range(2)}
    others = {0: swap(owned[0], "tp", 1)}
    ffn_last = fetch(ffn_low, (3,))

    def shaped(*arrays):
        return [x.reshape(8, -1, unit, x.shape[1]) for x in arrays]

    def land(total, chunk, first, second):
        rows = slot_rows(first, second, per_chunk)
        for at in range(per_chunk):
            h = order[chunk * per_chunk + at]
            total = total + (rows[at] if h == 0 else turn(rows[at], h)).astype(F32)
        return total

    kept = []
    folded = {}
    for chunk in range(CHUNKS):
        moving = []
        if chunk + 1 < CHUNKS:
            moving.append(("other", chunk + 1, [owned[chunk + 1]]))
        if chunk + 2 < CHUNKS:
            moving.append(("own", chunk + 2, list(started[chunk + 2])))
        if chunk + 3 < CHUNKS:
            moving.append(("start", chunk + 3, ffn_last))
        if chunk == 0:
            for n, group in enumerate(wide_near):
                moving.append(("other", f"near{n}", [group]))
            moving.append(("start", "far", wide_far))
        if chunk == 1:
            moving.append(("own", "far", list(started["far"])))
        if chunk == 2:
            moving.append(("other", "far", [owned["far"]]))
        for stage in range(3):
            if chunk - 1 - stage >= 0:
                moving.append((stage, chunk - 1 - stage, list(folded[chunk - 1 - stage])))
        flat = [x for entry in moving for x in entry[2]]
        rows_own, rows_other, *flat = tie(owned[chunk], others[chunk], *flat)
        results = []
        for name, c, values in moving:
            taken, flat = flat[: len(values)], flat[len(values) :]
            if name == "other":
                results.append([swap(taken[0], "tp", 1)])
            elif name == "own":
                results.append([spread_next(*taken)])
            elif name == "start":
                results.append(list(spread_start(taken)))
            else:
                results.append(list((collect_start, collect_next, collect_last)[name](*taken)))
        wide = (
            (wide_first, wide_first_other),
            (wide_near[0], others.get("near0")),
            (wide_near[-1], others.get("near1" if large else "near0")),
            (owned.get("far"), others.get("far")),
        )[chunk]
        outs = expert_pass(
            rows_own,
            rows_other,
            shaped(*wide),
            1 if chunk == 2 and not large else 0,
            chunk,
            slots_all,
            fixed,
            kept,
        )
        flat = [x for values in results for x in values]
        grad_keep, grad_send, *flat = tie(outs[0], outs[1], *flat)
        kept = outs[2:]
        for (name, c, _), values in zip(moving, results):
            taken, flat = flat[: len(values)], flat[len(values) :]
            if name == "other":
                others[c] = taken[0]
            elif name == "own":
                owned[c] = taken[0]
            elif name == "start":
                started[c] = taken
            else:
                folded[c] = taken
        folded[chunk] = [grad_keep, grad_send]
    d_ffn = land(jnp.zeros_like(x_mid), 0, *folded[0])
    d_ffn = land(d_ffn, 1, *collect_last(*folded[1]))
    d_ffn = land(d_ffn, 2, *collect_last(*collect_next(*folded[2])))
    d_ffn = land(d_ffn, 3, *collect_last(*collect_next(*collect_start(*folded[3]))))
    out_keep, out_send, rows_all, cotangent_rows, hidden_low, d_gate_low, d_up_low, dlog_low = [
        x.reshape(-1, x.shape[-1]) for x in kept
    ]
    def over_rows(left, right):
        return jnp.einsum("ta,tb->ab", left, right, preferred_element_type=F32)

    def split_experts(wide_grad):
        return wide_grad.reshape(-1, local_experts, hidden_width).transpose(1, 0, 2)

    d_ffn, out_keep, out_send = tie(d_ffn, out_keep, out_send)
    out_first, out_second = collect_start(out_keep, out_send)
    if large:
        out_first, out_second, rows_all, d_gate_low, d_up_low, hidden_low = tie(
            out_first, out_second, rows_all, d_gate_low, d_up_low, hidden_low
        )
        router_grad_t = over_rows(dlog_low, rows_all)
        down_grad = over_rows(hidden_low, cotangent_rows).reshape(expert_down.shape)
        gate_grad = split_experts(over_rows(rows_all, d_gate_low))
        up_grad = split_experts(over_rows(rows_all, d_up_low))
        d_ffn, router_grad_t, down_grad, gate_grad, up_grad = tie(
            d_ffn, router_grad_t, down_grad, gate_grad, up_grad
        )
    d_mid_norm, post_norm_grad = post_norm_back(d_ffn)
    d_mid = my_rows(out_grad).astype(F32) + d_mid_norm
    d_mid_low = join_rows(d_mid.astype(LOW))
    o_sum = jnp.einsum("tj,td->jd", o_low, d_mid_low, preferred_element_type=F32).astype(LOW)
    d_attn_low = jnp.einsum(
        "td,jd->tj", d_mid_low, o_weight, preferred_element_type=F32
    ).astype(LOW)
    d_attn_low, o_sum, out_first, out_second = tie(d_attn_low, o_sum, out_first, out_second)
    masks = ep_masks()
    o_sum = halve_sum(o_sum, masks[0])
    out_second = fold(out_second, "tp", 2)
    dq_low, dk_all, dv_all, q_gain_grad = attend_back(
        place, q_lin, d_attn_low, gain_row, cos, sin, k_all, v_all, inverse
    )
    dq_low, dk_all, dv_all, o_sum, out_first, out_second = tie(
        dq_low, dk_all, dv_all, o_sum, out_first, out_second
    )
    out_first = fold_inner(out_first, "tp", 2)
    for mask in masks[1:]:
        o_sum = halve_sum(o_sum, mask)
    split = dq_low.shape[1] // 2
    first_sum = jnp.einsum(
        "td,tj->dj", attn_low, dq_low[:, :split], preferred_element_type=F32
    ).astype(LOW)
    first_sum = halve_sum(first_sum, masks[0])
    pair_grad = jnp.concatenate([dk_all, dv_all], axis=1)
    total = pair_grad[:tokens]
    for d in range(1, SPAN):
        part = pair_grad[d * tokens : (d + 1) * tokens].astype(LOW)
        total = total + swap(part, "ep", d).astype(F32)
    dk_lin, k_gain_grad = k_back(total[:, :head_width])
    dk_low = dk_lin.astype(LOW)
    dv_low = total[:, head_width:].astype(LOW)
    second_sum = jnp.einsum(
        "td,tj->dj",
        attn_low,
        jnp.concatenate([dq_low[:, split:], dk_low, dv_low], axis=1),
        preferred_element_type=F32,
    ).astype(LOW)
    d_attn_in = jnp.einsum("tj,dj->td", dq_low, q_weight, preferred_element_type=F32)
    d_attn_in = d_attn_in + jnp.einsum("tj,dj->td", dk_low, k_weight, preferred_element_type=F32)
    d_attn_in = d_attn_in + jnp.einsum("tj,dj->td", dv_low, v_weight, preferred_element_type=F32)

    first_sum, second_sum, o_sum, d_attn_in, out_first, dlog_low, hidden_low = tie(
        first_sum, second_sum, o_sum, d_attn_in, out_first, dlog_low, hidden_low
    )
    second_sum = halve_sum(second_sum, masks[0])
    for mask in masks[1:]:
        first_sum = halve_sum(first_sum, mask)
    for mask in masks[:0:-1]:
        o_sum = double(o_sum, mask)
    d_attn_rows = sum_rows(d_attn_in)
    _, input_norm_back = jax.vjp(rms_scale, my_rows(x_full), input_norm)
    d_in_norm, input_norm_grad = input_norm_back(d_attn_rows)
    input_rows = (d_mid + d_in_norm).astype(LOW)
    if not large:
        router_grad_t = over_rows(dlog_low, rows_all)
        down_grad = over_rows(hidden_low, cotangent_rows).reshape(expert_down.shape)
    gains = jnp.concatenate([q_gain_grad.reshape(-1), k_gain_grad])
    small = jnp.concatenate(
        [
            router_grad_t,
            post_norm_grad[None],
            input_norm_grad[None],
            jnp.pad(gains, (0, model_width - gains.shape[0]))[None],
        ],
        axis=0,
    )
    first_sum, second_sum, o_sum, small, input_rows, d_gate_low, d_up_low = tie(
        first_sum, second_sum, o_sum, small, input_rows, d_gate_low, d_up_low
    )
    o_sum = double(o_sum, masks[0])
    for mask in masks[1:]:
        second_sum = halve_sum(second_sum, mask)
    for mask in masks[:0:-1]:
        first_sum = double(first_sum, mask)
    if not large:
        gate_grad = split_experts(over_rows(rows_all, d_gate_low))
    input_grad = join_rows(input_rows)
    first_sum, second_sum, o_sum, small, d_up_low, out_first, out_second = tie(
        first_sum, second_sum, o_sum, small, d_up_low, out_first, out_second
    )
    first_sum = double(first_sum, masks[0])
    for mask in masks[:0:-1]:
        second_sum = double(second_sum, mask)
    out_first, out_second = fold(out_first, "ep", 1), fold(out_second, "ep", 1)
    if not large:
        up_grad = split_experts(over_rows(rows_all, d_up_low))
    first_sum, second_sum, small, out_first, out_second = tie(
        first_sum, second_sum, small, out_first, out_second
    )
    second_sum = double(second_sum, masks[0])
    small = sum_all(small)
    out_slots = slot_rows(out_first, out_second, slots_all)
    mixed = out_slots[0].astype(F32)
    for p in range(1, slots_all):
        mixed = mixed + turn(out_slots[p], order[p]).astype(F32)
    block_rows = (x_mid + mixed).astype(LOW)
    block_out = lax.all_to_all(block_rows, "tp", split_axis=1, concat_axis=0, tiled=True)
    o_weight_grad = o_sum.astype(F32)
    q_weight_grad = jnp.concatenate([first_sum, second_sum[:, :split]], axis=1).astype(F32)
    k_weight_grad = second_sum[:, split : split + head_width].astype(F32)
    v_weight_grad = second_sum[:, split + head_width :].astype(F32)
    router_grad = small[:experts_all].T
    post_norm_grad, input_norm_grad, gains = small[experts_all : experts_all + 3]
    return (
        block_out,
        input_grad,
        input_norm_grad,
        q_weight_grad,
        k_weight_grad,
        v_weight_grad,
        gains[:head_width],
        gains[head_width : 2 * head_width],
        o_weight_grad,
        post_norm_grad,
        router_grad,
        gate_grad,
        up_grad,
        down_grad,
    )


def solution(mesh):
    in_specs = (
        P("ep", None),
        P(),
        P(None, "tp"),
        P(None, "tp"),
        P(None, "tp"),
        P(),
        P(),
        P("tp", None),
        P(),
        P(),
        P("ep", None, "tp"),
        P("ep", None, "tp"),
        P("ep", "tp", None),
        P("ep", None),
        P(),
        P("ep", None),
    )
    out_specs = (
        P("ep", "tp"),
        P("ep", None),
        P(),
        P(None, "tp"),
        P(None, "tp"),
        P(None, "tp"),
        P(),
        P(),
        P("tp", None),
        P(),
        P(),
        P("ep", None, "tp"),
        P("ep", None, "tp"),
        P("ep", "tp", None),
    )
    return jax.shard_map(body, mesh=mesh, in_specs=in_specs, out_specs=out_specs, check_vma=False)
```

```python
import functools

import jax
import jax.numpy as jnp
from jax import lax
from jax.experimental import pallas as pl
from jax.experimental.pallas import tpu as pltpu
from jax.sharding import PartitionSpec as P

SPAN = 4
EPSILON = 1e-06
THETA = 1000000.0
MASKED = -1e30
LOG2E = 1.4426950408889634
NT_DIMS = (((1,), (1,)), ((), ()))
TN_DIMS = (((0,), (0,)), ((), ()))
VMEM_LIMIT = 60 * 1024 * 1024
TILE = 256
CHUNKS = 4
F32 = jnp.float32
LOW = jnp.bfloat16


def rms_scale(values, scales):
    return values * lax.rsqrt(jnp.mean(values * values, axis=-1, keepdims=True) + EPSILON) * scales


def swap(block, axis, mask):
    devices = range(lax.axis_size(axis))
    return lax.ppermute(block, axis, [(i, i ^ mask) for i in devices])


def turn(block, step):
    count = lax.axis_size("ep")
    return lax.ppermute(block, "ep", [(i, (i + 2 * step) % count) for i in range(count)])


def add_low(kept, received):
    return (kept.astype(F32) + received.astype(F32)).astype(LOW)


def halves(block):
    size = block.shape[0] // 2
    return block[:size], block[size:]


def spread_start(slots):
    half = slots[0].shape[0] // 2
    first = jnp.concatenate([rows[:half] for rows in slots], axis=0)
    second = jnp.concatenate([rows[half:] for rows in slots], axis=0)
    sends = [(first, "tp", 2), (second, "ep", 1)]
    return sends, lambda a, b: (jnp.concatenate([first, a]), jnp.concatenate([second, b]))


def spread_next(pair):
    first, second = pair
    sends = [(first, "ep", 1), (second, "tp", 2)]
    return sends, lambda a, b: jnp.concatenate([first, a, second, b])


def spread_last(own):
    return [(own, "tp", 1)], lambda a: a


def collect_start(kept, sent):
    return [(sent, "tp", 1)], lambda a: halves(add_low(kept, a))


def collect_both(pair, first_link, second_link):
    (first, first_sent), (second, second_sent) = halves(pair[0]), halves(pair[1])
    sends = [(first_sent, *first_link), (second_sent, *second_link)]
    return sends, lambda a, b: (add_low(first, a), add_low(second, b))


def collect_next(pair):
    return collect_both(pair, ("ep", 1), ("tp", 2))


def collect_last(pair):
    return collect_both(pair, ("tp", 2), ("ep", 1))


def fold_one(block, axis, mask):
    kept, sent = halves(block)
    return [(sent, axis, mask)], lambda a: add_low(kept, a)


def fold_inner(block, axis, mask):
    parts = block.reshape(2, 2, -1, block.shape[1])
    kept, sent = parts[:, 0], parts[:, 1]
    return [(sent, axis, mask)], lambda a: add_low(kept, a).reshape(-1, block.shape[1])


def tie(*values):
    return lax.optimization_barrier(values)


def now(stage):
    return stage[1](*[swap(x, axis, mask) for x, axis, mask in stage[0]])


def step(stages, compute=None, values=()):
    sends = [[send[0] for send in stage[0]] for stage in stages]
    sends, values = lax.optimization_barrier((sends, values))
    received = [
        [swap(x, axis, mask) for x, (_, axis, mask) in zip(blocks, stage[0])]
        for blocks, stage in zip(sends, stages)
    ]
    result = compute(*values) if compute is not None else values
    received, result = lax.optimization_barrier((received, result))
    return [stage[1](*blocks) for stage, blocks in zip(stages, received)], result


def slot_rows(first, second, count):
    parts = [part.reshape(count, -1, part.shape[1]) for part in (first, second)]
    return jnp.concatenate(parts, axis=1)


def pick(array, index, axis=0):
    return lax.dynamic_index_in_dim(array, index, axis, keepdims=False)


def ep_masks():
    return [1 << n for n in range(lax.axis_size("ep").bit_length() - 1)]


def halve_sum(block, mask):
    bit = lax.axis_index("ep") // mask % 2
    parts = block.reshape(2, -1, block.shape[1])
    kept, sent = pick(parts, bit), pick(parts, 1 - bit)
    return [(sent, "ep", mask)], lambda a: add_low(kept, a)


def double(block, mask):
    bit = lax.axis_index("ep") // mask % 2

    def join(other):
        low = jnp.where(bit == 0, block, other)
        high = jnp.where(bit == 0, other, block)
        return jnp.concatenate([low, high], axis=0)

    return [(block, "ep", mask)], join


def sum_axis(values, axis):
    mask = 1
    while mask < lax.axis_size(axis):
        values = values + swap(values, axis, mask)
        mask *= 2
    return values


def sum_tp(values):
    return sum_axis(values, "tp")


def sum_over_ep(values):
    return sum_axis(values, "ep")


def expert_kernel(
    own_ref,
    other_ref,
    cotangent_own_ref,
    cotangent_other_ref,
    router_ref,
    router_t_ref,
    select_ref,
    gate_ref,
    up_ref,
    down_ref,
    *refs,
):
    grad_keep_ref, grad_send_ref, out_keep_ref, out_send_ref = refs[-10:-6]
    rows_ref, cotangents_ref, hidden_ref, d_gate_ref, d_up_ref, dlog_ref = refs[-6:]
    is_own = pl.program_id(0) < pl.num_programs(0) // 2
    rows = jnp.where(is_own, own_ref[...], other_ref[...])
    model_width = rows.shape[1]
    cotangents = jnp.where(is_own, cotangent_own_ref[...], cotangent_other_ref[...])
    cotangents = cotangents.reshape(rows.shape[0], -1)
    chosen = cotangents[:, model_width : model_width + router_ref.shape[1]].astype(F32)
    logits = jnp.dot(rows, router_ref[...], preferred_element_type=F32)
    logits = jnp.where(chosen > 0.5, logits, MASKED)
    probs = jnp.exp(logits - jnp.max(logits, axis=-1, keepdims=True))
    probs = probs / jnp.sum(probs, axis=-1, keepdims=True)
    select = select_ref[...]
    probs_high = probs.astype(LOW)
    probs_rest = (probs - probs_high.astype(F32)).astype(LOW)
    weight = jnp.dot(probs_high, select, preferred_element_type=F32)
    weight += jnp.dot(probs_rest, select, preferred_element_type=F32)
    gate = jnp.dot(rows, gate_ref[...], preferred_element_type=F32)
    up = jnp.dot(rows, up_ref[...], preferred_element_type=F32)
    d_hidden = (
        lax.dot_general(
            cotangents[:, :model_width], down_ref[...], NT_DIMS, preferred_element_type=F32
        )
        * weight
    )
    sig = 1.0 / (1.0 + jnp.exp(-gate))
    silu = gate * sig
    hidden = silu * up
    d_up = (d_hidden * silu).astype(LOW)
    d_gate = (d_hidden * up * sig * (1.0 + gate * (1.0 - sig))).astype(LOW)
    hidden_low = (hidden * weight).astype(LOW)
    dots = lax.dot_general(
        (d_hidden * hidden).astype(LOW), select, NT_DIMS, preferred_element_type=F32
    )
    dlog = (dots - probs * jnp.sum(dots, axis=-1, keepdims=True)).astype(LOW)

    def store(ref, values):
        ref[...] = values.reshape(ref.shape)

    def store_either(keep_ref, send_ref, values):
        @pl.when(is_own)
        def _():
            store(keep_ref, values)

        @pl.when(jnp.logical_not(is_own))
        def _():
            store(send_ref, values)

    store(rows_ref, rows)
    store(cotangents_ref, cotangents[:, :model_width])
    store(hidden_ref, hidden_low)
    store(d_gate_ref, d_gate)
    store(d_up_ref, d_up)
    store(dlog_ref, dlog)
    outs = jnp.dot(hidden_low, down_ref[...], preferred_element_type=F32).astype(LOW)
    store_either(out_keep_ref, out_send_ref, outs)
    grads = lax.dot_general(d_gate, gate_ref[...], NT_DIMS, preferred_element_type=F32)
    grads += lax.dot_general(d_up, up_ref[...], NT_DIMS, preferred_element_type=F32)
    grads += jnp.dot(dlog, router_t_ref[...], preferred_element_type=F32)
    store_either(grad_keep_ref, grad_send_ref, grads.astype(LOW))


def expert_pass(own, other, cotangents, at, chunk, slots_all, fixed, kept):
    count, model_width = own.shape
    groups, _, unit, wide = cotangents[0].shape
    slots = slots_all // CHUNKS
    half = count // TILE
    width = fixed[-1].shape[0]
    experts_all = fixed[0].shape[1]
    block = TILE // (slots * unit)

    def first(i):
        return jnp.minimum(i, half - 1)

    def second(i):
        return jnp.maximum(i - half, 0)

    def every(i):
        return i

    def rows_spec(index):
        return pl.BlockSpec((TILE, model_width), lambda i: (index(i), 0))

    def placed(columns, index, where):
        return pl.BlockSpec((block, slots, unit, columns), lambda i: (index(i), where, 0, 0))

    def whole(array):
        return pl.BlockSpec(array.shape, lambda i: (0, 0), pipeline_mode=pl.Buffered(1))

    columns = (model_width, model_width, width, width, width, experts_all)
    in_specs = [
        rows_spec(first),
        rows_spec(second),
        placed(wide, first, at),
        placed(wide, second, at),
    ] + [whole(array) for array in fixed]
    loose = 4 if slots_all > CHUNKS else 2
    aliases = {len(in_specs) + n: loose + n for n in range(len(kept))}
    part = jax.ShapeDtypeStruct((count, model_width), LOW)
    place = jax.ShapeDtypeStruct((groups, slots_all, unit, model_width), LOW)
    return pl.pallas_call(
        expert_kernel,
        grid=(2 * half,),
        in_specs=in_specs + [pl.BlockSpec(memory_space=pl.ANY)] * len(kept),
        out_specs=[rows_spec(first), rows_spec(second)]
        + (
            [rows_spec(first), rows_spec(second)]
            if loose == 4
            else [placed(model_width, first, chunk), placed(model_width, second, chunk)]
        )
        + [placed(size, every, chunk) for size in columns],
        out_shape=[part, part]
        + ([part, part] if loose == 4 else [place, place])
        + [jax.ShapeDtypeStruct((2 * groups, slots_all, unit, size), LOW) for size in columns],
        input_output_aliases=aliases,
        compiler_params=pltpu.CompilerParams(vmem_limit_bytes=VMEM_LIMIT),
        cost_estimate=pl.CostEstimate(
            flops=24 * count * model_width * width,
            bytes_accessed=20 * count * model_width,
            transcendentals=2 * count * width,
        ),
        name="expert_pass",
    )(own, other, *cotangents, *fixed, *kept)


def turned_halves(values):
    return pltpu.roll(values, values.shape[1] // 2, 1)


def head_rows(lin, gain, cos, sin):
    scale = lax.rsqrt(jnp.mean(lin * lin, axis=-1, keepdims=True) + EPSILON)
    hat = lin * scale
    normed = hat * gain
    return scale, hat, normed * cos + turned_halves(normed) * sin


def allowed_keys(place_ref, block, keys, queries):
    key_pos = place_ref[2 + block] + lax.broadcasted_iota(jnp.int32, (keys, 1), 0)
    key_pos = jnp.where(key_pos < place_ref[1], -1, key_pos)
    query_pos = place_ref[0] + lax.broadcasted_iota(jnp.int32, (1, queries), 1)
    return key_pos <= query_pos


def attend_kernel(
    place_ref, q_ref, gain_ref, cos_ref, sin_ref, k_ref, v_t_ref, o_ref, norm_ref
):
    queries, head_width = q_ref.shape
    _, _, q_rot = head_rows(q_ref[...], gain_ref[...], cos_ref[...], sin_ref[...])
    q_low = q_rot.astype(LOW)
    factor = head_width ** (-0.5) * LOG2E
    total = jnp.zeros((1, queries), F32)
    acc = jnp.zeros((head_width, queries), F32)
    for block in range(SPAN):
        span = pl.ds(block * queries, queries)
        scores = lax.dot_general(k_ref[span, :], q_low, NT_DIMS, preferred_element_type=F32)
        probs = jnp.where(
            allowed_keys(place_ref, block, queries, queries), jnp.exp2(scores * factor), 0.0
        )
        total += jnp.sum(probs, axis=0, keepdims=True)
        acc += jnp.dot(v_t_ref[:, span], probs.astype(LOW), preferred_element_type=F32)
    o_ref[...] = (acc / total).T.astype(LOW)
    norm_ref[0] = 1.0 / total


def attend(place, q_lin, gain, cos, sin, k_all, v_t):
    tokens, columns = q_lin.shape
    head_width = gain.shape[1]
    heads = columns // head_width
    row = pl.BlockSpec((tokens, head_width), lambda h, p: (0, h))

    def whole(array):
        return pl.BlockSpec(array.shape, lambda h, p: (0, 0))

    return pl.pallas_call(
        attend_kernel,
        grid_spec=pltpu.PrefetchScalarGridSpec(
            num_scalar_prefetch=1,
            grid=(heads,),
            in_specs=[row] + [whole(x) for x in (gain, cos, sin, k_all, v_t)],
            out_specs=[row, pl.BlockSpec((1, 1, tokens), lambda h, p: (h, 0, 0))],
        ),
        out_shape=[
            jax.ShapeDtypeStruct((tokens, columns), LOW),
            jax.ShapeDtypeStruct((heads, 1, tokens), F32),
        ],
        compiler_params=pltpu.CompilerParams(vmem_limit_bytes=VMEM_LIMIT),
        cost_estimate=pl.CostEstimate(
            flops=16 * SPAN * tokens * tokens * columns // 8 * 2,
            bytes_accessed=8 * tokens * columns,
            transcendentals=SPAN * tokens * tokens * heads,
        ),
        name="attend",
    )(place, q_lin, gain, cos, sin, k_all, v_t)


def attend_back_kernel(
    place_ref,
    q_ref,
    d_ref,
    gain_ref,
    cos_ref,
    sin_ref,
    k_ref,
    k_t_ref,
    v_ref,
    norm_ref,
    dq_ref,
    dk_ref,
    dv_ref,
    dgain_ref,
):
    queries, head_width = q_ref.shape
    gain = gain_ref[...]
    scale, hat, q_rot = head_rows(q_ref[...], gain, cos_ref[...], sin_ref[...])
    q_low = q_rot.astype(LOW)
    d_low = d_ref[...]
    shrink = head_width ** (-0.5)
    factor = shrink * LOG2E
    inverse = norm_ref[0]
    delta = jnp.zeros((1, queries), F32)
    kept = []

    @pl.when(pl.program_id(0) == 0)
    def _():
        dk_ref[...] = jnp.zeros_like(dk_ref)
        dv_ref[...] = jnp.zeros_like(dv_ref)
        dgain_ref[...] = jnp.zeros_like(dgain_ref)

    for block in range(SPAN):
        span = pl.ds(block * queries, queries)
        scores = lax.dot_general(k_ref[span, :], q_low, NT_DIMS, preferred_element_type=F32)
        probs = jnp.where(
            allowed_keys(place_ref, block, queries, queries),
            jnp.exp2(scores * factor) * inverse,
            0.0,
        )
        d_probs = lax.dot_general(v_ref[span, :], d_low, NT_DIMS, preferred_element_type=F32)
        delta += jnp.sum(probs * d_probs, axis=0, keepdims=True)
        dv_ref[span, :] += jnp.dot(probs.astype(LOW), d_low, preferred_element_type=F32)
        kept.append((probs, d_probs))
    acc = jnp.zeros((head_width, queries), F32)
    for block in range(SPAN):
        span = pl.ds(block * queries, queries)
        probs, d_probs = kept[block]
        d_scores = (probs * (d_probs - delta)).astype(LOW)
        dk_ref[span, :] += jnp.dot(d_scores, q_low, preferred_element_type=F32) * shrink
        acc += jnp.dot(k_t_ref[:, span], d_scores, preferred_element_type=F32)
    d_rot = acc.T * shrink
    d_normed = d_rot * cos_ref[...] + turned_halves(d_rot * sin_ref[...])
    dgain_ref[...] += jnp.sum(d_normed * hat, axis=0, keepdims=True)
    scaled = d_normed * gain
    d_lin = scale * (scaled - hat * jnp.mean(scaled * hat, axis=-1, keepdims=True))
    dq_ref[...] = d_lin.astype(LOW)


def attend_back(place, q_lin, d_attn, gain, cos, sin, k_all, v_all, inverse):
    tokens, columns = q_lin.shape
    head_width = gain.shape[1]
    heads = columns // head_width
    keys = k_all.shape[0]
    row = pl.BlockSpec((tokens, head_width), lambda h, p: (0, h))
    k_t = k_all.T

    def whole(shape):
        return pl.BlockSpec(shape, lambda h, p: (0, 0))

    fixed = (gain, cos, sin, k_all, k_t, v_all)
    return pl.pallas_call(
        attend_back_kernel,
        grid_spec=pltpu.PrefetchScalarGridSpec(
            num_scalar_prefetch=1,
            grid=(heads,),
            in_specs=[row, row]
            + [whole(x.shape) for x in fixed]
            + [pl.BlockSpec((1, 1, tokens), lambda h, p: (h, 0, 0))],
            out_specs=[
                row,
                whole((keys, head_width)),
                whole((keys, head_width)),
                whole((1, head_width)),
            ],
        ),
        out_shape=[
            jax.ShapeDtypeStruct((tokens, columns), LOW),
            jax.ShapeDtypeStruct((keys, head_width), F32),
            jax.ShapeDtypeStruct((keys, head_width), F32),
            jax.ShapeDtypeStruct((1, head_width), F32),
        ],
        compiler_params=pltpu.CompilerParams(vmem_limit_bytes=VMEM_LIMIT),
        cost_estimate=pl.CostEstimate(
            flops=20 * keys * tokens * columns,
            bytes_accessed=8 * tokens * columns,
            transcendentals=keys * tokens * heads,
        ),
        name="attend_back",
    )(place, q_lin, d_attn, *fixed, inverse)


def body(
    block_in,
    input_norm,
    q_weight,
    k_weight,
    v_weight,
    q_gain,
    k_gain,
    o_weight,
    post_norm,
    router,
    expert_gate,
    expert_up,
    expert_down,
    expert_ids,
    prefix_len,
    out_grad,
):
    tokens, model_width = block_in.shape
    head_width = q_gain.shape[0]
    tp_count = lax.axis_size("tp")
    tp_rank = lax.axis_index("tp")
    ep_count = lax.axis_size("ep")
    ep_rank = lax.axis_index("ep")
    share_rows = tokens // tp_count
    dev_slot = ep_rank % SPAN
    prefix = lax.dynamic_index_in_dim(prefix_len, ep_rank // SPAN, keepdims=False)
    core_bit = tp_rank % 2
    x_bit = tp_rank // 2
    row_index = jnp.arange(tokens, dtype=jnp.int32)
    slots_all = ep_count // 2

    def block_place(slot):
        return (slot + SPAN - 1) % SPAN * tokens

    def my_rows(full_rows):
        return lax.dynamic_slice_in_dim(full_rows, tp_rank * share_rows, share_rows, 0)

    def sum_rows(partial_rows):
        parts = partial_rows.reshape(2, 2, share_rows, -1)

        sent = swap(pick(parts, 1 - core_bit, 1).astype(LOW), "tp", 1)
        parts = pick(parts, core_bit, 1) + sent.astype(F32)
        sent = swap(pick(parts, 1 - x_bit, 0).astype(LOW), "tp", 2)
        return pick(parts, x_bit, 0) + sent.astype(F32)

    def join_rows(rows):
        other = swap(rows, "tp", 2)
        pair = jnp.stack([jnp.where(x_bit == 0, rows, other), jnp.where(x_bit == 0, other, rows)])
        other = swap(pair, "tp", 1)
        low = jnp.where(core_bit == 0, pair, other)
        high = jnp.where(core_bit == 0, other, pair)
        return jnp.stack([low, high], axis=1).reshape(tokens, -1)

    experts_all = router.shape[1]
    local_experts = expert_gate.shape[0]
    hidden_width = expert_gate.shape[2]
    expert_index = jnp.arange(experts_all, dtype=jnp.int32)
    width = local_experts * hidden_width

    chosen = jnp.any(my_rows(expert_ids)[:, :, None] == expert_index[None, None, :], axis=1)
    chosen = jnp.pad(chosen.astype(LOW), ((0, 0), (0, -experts_all % 128)))
    wide_rows = jnp.concatenate([my_rows(out_grad), chosen], axis=1)
    per_chunk = slots_all // CHUNKS
    order = [c * per_chunk + at for c in (0, 1, 3, 2) for at in range(per_chunk)]
    unit = share_rows // 2

    def fetch(rows, positions):
        return [
            rows if order[p] == 0 else turn(rows, slots_all - order[p])
            for c in positions
            for p in range(c * per_chunk, (c + 1) * per_chunk)
        ]

    large = slots_all > CHUNKS
    groups = ((0,), (1,), (2,), (3,)) if large else ((0,), (1, 2), (3,))
    wide_first = now(spread_start(fetch(wide_rows, groups[0])))
    wide_near = [fetch(wide_rows, group) for group in groups[1:-1]]

    x_full = block_in.astype(F32)
    attn_low = rms_scale(x_full, input_norm).astype(LOW)
    k_lin = jnp.dot(attn_low, k_weight, preferred_element_type=F32)
    v_low = jnp.dot(attn_low, v_weight, preferred_element_type=F32).astype(LOW)
    half_width = head_width // 2
    exponents = jnp.arange(half_width, dtype=F32) * (-2.0 / head_width)
    positions = block_place(dev_slot) + row_index
    angles = positions.astype(F32)[:, None] * (THETA**exponents)[None, :]
    cos_half, sin_half = jnp.cos(angles), jnp.sin(angles)
    cos = jnp.concatenate([cos_half, cos_half], axis=1)
    sin = jnp.concatenate([-sin_half, sin_half], axis=1)

    def key_path(lin_rows, scales):
        normed = rms_scale(lin_rows, scales)
        lead, tail = normed[:, :half_width], normed[:, half_width:]
        return normed * cos + jnp.concatenate([tail, lead], axis=1) * sin

    k_rot, k_back = jax.vjp(key_path, k_lin, k_gain)
    pair = jnp.concatenate([k_rot.astype(LOW), v_low], axis=1)
    pair, wide_first = tie(pair, wide_first)
    pairs = [pair] + [swap(pair, "ep", d) for d in range(1, SPAN)]
    wide_first = now(spread_next(wide_first))
    q_lin = jnp.dot(attn_low, q_weight, preferred_element_type=F32)
    gate_cat = expert_gate.transpose(1, 0, 2).reshape(-1, width)
    up_cat = expert_up.transpose(1, 0, 2).reshape(-1, width)
    gate_cat, up_cat, q_lin, wide_first, wide_rows, pairs, wide_near = tie(
        gate_cat, up_cat, q_lin, wide_first, wide_rows, pairs, wide_near
    )
    wide_far = fetch(wide_rows, groups[-1])
    wide_near = [now(spread_start(group)) for group in wide_near]
    wide_first_other = now(spread_last(wide_first))
    k_all = jnp.concatenate([p[:, :head_width] for p in pairs], axis=0)
    v_all = jnp.concatenate([p[:, head_width:] for p in pairs], axis=0)
    place = jnp.stack(
        [block_place(dev_slot), prefix] + [block_place(dev_slot ^ d) for d in range(SPAN)]
    ).astype(jnp.int32)
    gain_row = q_gain.reshape(1, -1)
    o_low, inverse = attend(place, q_lin, gain_row, cos, sin, k_all, v_all.T)
    o_low, wide_first_other, wide_near = tie(o_low, wide_first_other, wide_near)
    wide_near = [now(spread_next(group)) for group in wide_near]
    head_part = jnp.dot(o_low, o_weight, preferred_element_type=F32)
    x_mid = my_rows(x_full) + sum_rows(head_part)
    ffn_in, post_norm_back = jax.vjp(rms_scale, x_mid, post_norm)
    ffn_low = ffn_in.astype(LOW)
    ffn_low, wide_far = tie(ffn_low, wide_far)

    own_expert = ep_rank * local_experts + jnp.arange(width, dtype=jnp.int32) // hidden_width
    select = (expert_index[:, None] == own_expert[None, :]).astype(LOW)
    down_cat = expert_down.reshape(width, -1)
    fixed = (router, router.T, select, gate_cat, up_cat, down_cat)
    started = {c: now(spread_start(fetch(ffn_low, (c,)))) for c in range(3)}
    owned = {c: now(spread_next(started[c])) for c in range(2)}
    others = {0: now(spread_last(owned[0])), "wide0": wide_first_other}
    owned["wide0"] = wide_first
    for n, group in enumerate(wide_near):
        owned[f"wide{n + 1}"] = group
    ffn_last = fetch(ffn_low, (3,))

    def shaped(*arrays):
        return [x.reshape(8, -1, unit, x.shape[1]) for x in arrays]

    def apply_experts(at, chunk, own, other, wide_own, wide_other, *kept):
        wide = shaped(wide_own, wide_other)
        return expert_pass(own, other, wide, at, chunk, slots_all, fixed, kept)

    def land(total, chunk, pair):
        rows = slot_rows(*pair, per_chunk)
        for at in range(per_chunk):
            h = order[chunk * per_chunk + at]
            total = total + (rows[at] if h == 0 else turn(rows[at], h)).astype(F32)
        return total

    kept = []
    back, forth = {}, {}
    for chunk in range(CHUNKS):
        names, stages = [], []

        def add(store, key, stage):
            names.append((store, key))
            stages.append(stage)

        if chunk + 1 < CHUNKS:
            add(others, chunk + 1, spread_last(owned[chunk + 1]))
        if chunk + 2 < CHUNKS:
            add(owned, chunk + 2, spread_next(started[chunk + 2]))
        if chunk == 0:
            add(started, 3, spread_start(ffn_last))
            add(started, "far", spread_start(wide_far))
        for n, group in enumerate(groups):
            if group == (3,) and chunk == 1:
                add(owned, f"wide{n}", spread_next(started["far"]))
            if chunk == group[0] - 1:
                add(others, f"wide{n}", spread_last(owned[f"wide{n}"]))
        for store in (back, forth) if large else (back,):
            if chunk >= 1:
                add(store, chunk - 1, collect_start(*store[chunk - 1]))
            if chunk >= 2:
                add(store, chunk - 2, collect_next(store[chunk - 2]))
            if chunk >= 3:
                add(store, chunk - 3, collect_last(store[chunk - 3]))
        n, group = next((n, group) for n, group in enumerate(groups) if chunk in group)
        wide = owned[f"wide{n}"], others[f"wide{n}"]
        at = chunk - group[0]
        results, outs = step(
            stages,
            functools.partial(apply_experts, at, chunk),
            (owned[chunk], others[chunk], *wide, *kept),
        )
        for (store, key), value in zip(names, results):
            store[key] = value
        back[chunk] = outs[:2]
        forth[chunk] = outs[2:4]
        kept = outs[4:] if large else outs[2:]
    rows_all, cotangent_rows, hidden_low, d_gate_low, d_up_low, dlog_low = [
        x.reshape(-1, x.shape[-1]) for x in kept[-6:]
    ]
    if large:
        forth[3] = now(collect_start(*forth[3]))
        forth[2], forth[3] = [now(collect_next(forth[c])) for c in (2, 3)]
        for c in (1, 2, 3):
            forth[c] = now(collect_last(forth[c]))
        out_pair = [jnp.concatenate([forth[c][n] for c in range(CHUNKS)]) for n in range(2)]
        out_pair, rows_all, back = tie(out_pair, rows_all, back)
    else:
        out_keep, out_send = [x.reshape(-1, model_width) for x in kept[:2]]

    def over_rows(left, right):
        return jnp.einsum("ta,tb->ab", left, right, preferred_element_type=F32)

    def split_experts(wide_grad):
        return wide_grad.reshape(-1, local_experts, hidden_width).transpose(1, 0, 2)

    d_ffn = land(jnp.zeros_like(x_mid), 0, back[0])
    (back[1], back[2], back[3]), down_grad = step(
        [collect_last(back[1]), collect_next(back[2]), collect_start(*back[3])],
        over_rows,
        (hidden_low, cotangent_rows),
    )
    down_grad = down_grad.reshape(expert_down.shape)
    d_ffn = land(d_ffn, 1, back[1])
    (back[2], back[3]), gate_grad = step(
        [collect_last(back[2]), collect_next(back[3])], over_rows, (rows_all, d_gate_low)
    )
    d_ffn = land(d_ffn, 2, back[2])
    (back[3],), router_grad_t = step([collect_last(back[3])], over_rows, (dlog_low, rows_all))
    d_ffn = land(d_ffn, 3, back[3])

    d_mid_norm, post_norm_grad = post_norm_back(d_ffn)
    d_mid = my_rows(out_grad).astype(F32) + d_mid_norm
    if large:
        d_mid_low = join_rows(d_mid.astype(LOW))
    else:
        (out_pair,), d_mid_low = step(
            [collect_start(out_keep, out_send)], join_rows, (d_mid.astype(LOW),)
        )
    o_sum = jnp.einsum("tj,td->jd", o_low, d_mid_low, preferred_element_type=F32).astype(LOW)
    d_attn_low = jnp.einsum(
        "td,jd->tj", d_mid_low, o_weight, preferred_element_type=F32
    ).astype(LOW)
    masks = ep_masks()
    out_first, out_second = out_pair
    d_attn_low, o_sum, out_first, out_second = tie(d_attn_low, o_sum, out_first, out_second)
    o_sum = now(halve_sum(o_sum, masks[0]))
    if not large:
        out_second = now(fold_one(out_second, "tp", 2))
    dq_low, dk_all, dv_all, q_gain_grad = attend_back(
        place, q_lin, d_attn_low, gain_row, cos, sin, k_all, v_all, inverse
    )
    dq_low, dk_all, dv_all, o_sum, out_first, out_second = tie(
        dq_low, dk_all, dv_all, o_sum, out_first, out_second
    )
    if not large:
        out_first = now(fold_inner(out_first, "tp", 2))
    for mask in masks[1:]:
        o_sum = now(halve_sum(o_sum, mask))
    split = dq_low.shape[1] // 2
    first_sum = jnp.einsum(
        "td,tj->dj", attn_low, dq_low[:, :split], preferred_element_type=F32
    ).astype(LOW)
    first_sum = now(halve_sum(first_sum, masks[0]))
    pair_grad = jnp.concatenate([dk_all, dv_all], axis=1)
    total = pair_grad[:tokens]
    for d in range(1, SPAN):
        part = pair_grad[d * tokens : (d + 1) * tokens].astype(LOW)
        total = total + swap(part, "ep", d).astype(F32)
    dk_lin, k_gain_grad = k_back(total[:, :head_width])
    dk_low = dk_lin.astype(LOW)
    dv_low = total[:, head_width:].astype(LOW)
    second_sum = jnp.einsum(
        "td,tj->dj",
        attn_low,
        jnp.concatenate([dq_low[:, split:], dk_low, dv_low], axis=1),
        preferred_element_type=F32,
    ).astype(LOW)
    d_attn_in = jnp.einsum("tj,dj->td", dq_low, q_weight, preferred_element_type=F32)
    d_attn_in = d_attn_in + jnp.einsum("tj,dj->td", dk_low, k_weight, preferred_element_type=F32)
    d_attn_in = d_attn_in + jnp.einsum("tj,dj->td", dv_low, v_weight, preferred_element_type=F32)

    second_sum = now(halve_sum(second_sum, masks[0]))
    for mask in masks[1:]:
        first_sum = now(halve_sum(first_sum, mask))
    for mask in masks[:0:-1]:
        o_sum = now(double(o_sum, mask))
    d_attn_rows = sum_rows(d_attn_in)
    _, input_norm_back = jax.vjp(rms_scale, my_rows(x_full), input_norm)
    d_in_norm, input_norm_grad = input_norm_back(d_attn_rows)
    input_rows = (d_mid + d_in_norm).astype(LOW)
    gains = jnp.concatenate([q_gain_grad.reshape(-1), k_gain_grad])
    small = jnp.concatenate(
        [
            router_grad_t,
            post_norm_grad[None],
            input_norm_grad[None],
            jnp.pad(gains, (0, model_width - gains.shape[0]))[None],
        ],
        axis=0,
    )
    first_sum, second_sum, o_sum, small, input_rows, out_first, out_second, gate_grad = tie(
        first_sum, second_sum, o_sum, small, input_rows, out_first, out_second, gate_grad
    )
    o_sum = now(double(o_sum, masks[0]))
    for mask in masks[1:]:
        second_sum = now(halve_sum(second_sum, mask))
    for mask in masks[:0:-1]:
        first_sum = now(double(first_sum, mask))
    up_grad = over_rows(rows_all, d_up_low)
    small = sum_tp(small)
    input_grad = join_rows(input_rows)
    first_sum, second_sum, o_sum, small, up_grad, out_first, out_second = tie(
        first_sum, second_sum, o_sum, small, up_grad, out_first, out_second
    )
    first_sum = now(double(first_sum, masks[0]))
    for mask in masks[:0:-1]:
        second_sum = now(double(second_sum, mask))
    if not large:
        out_first = now(fold_one(out_first, "ep", 1))
        out_second = now(fold_one(out_second, "ep", 1))
    first_sum, second_sum, small, out_first, out_second, gate_grad, up_grad = tie(
        first_sum, second_sum, small, out_first, out_second, gate_grad, up_grad
    )
    second_sum = now(double(second_sum, masks[0]))
    small = sum_over_ep(small)
    gate_grad, up_grad = split_experts(gate_grad), split_experts(up_grad)
    out_slots = slot_rows(out_first, out_second, slots_all)
    mixed = out_slots[0].astype(F32)
    for p in range(1, slots_all):
        mixed = mixed + turn(out_slots[p], order[p]).astype(F32)
    block_rows = (x_mid + mixed).astype(LOW)
    block_out = lax.all_to_all(block_rows, "tp", split_axis=1, concat_axis=0, tiled=True)
    o_weight_grad = o_sum.astype(F32)
    q_weight_grad = jnp.concatenate([first_sum, second_sum[:, :split]], axis=1).astype(F32)
    k_weight_grad = second_sum[:, split : split + head_width].astype(F32)
    v_weight_grad = second_sum[:, split + head_width :].astype(F32)
    router_grad = small[:experts_all].T
    post_norm_grad, input_norm_grad, gains = small[experts_all : experts_all + 3]
    return (
        block_out,
        input_grad,
        input_norm_grad,
        q_weight_grad,
        k_weight_grad,
        v_weight_grad,
        gains[:head_width],
        gains[head_width : 2 * head_width],
        o_weight_grad,
        post_norm_grad,
        router_grad,
        gate_grad,
        up_grad,
        down_grad,
    )


def solution(mesh):
    in_specs = (
        P("ep", None),
        P(),
        P(None, "tp"),
        P(None, "tp"),
        P(None, "tp"),
        P(),
        P(),
        P("tp", None),
        P(),
        P(),
        P("ep", None, "tp"),
        P("ep", None, "tp"),
        P("ep", "tp", None),
        P("ep", None),
        P(),
        P("ep", None),
    )
    out_specs = (
        P("ep", "tp"),
        P("ep", None),
        P(),
        P(None, "tp"),
        P(None, "tp"),
        P(None, "tp"),
        P(),
        P(),
        P("tp", None),
        P(),
        P(),
        P("ep", None, "tp"),
        P("ep", None, "tp"),
        P("ep", "tp", None),
    )
    return jax.shard_map(body, mesh=mesh, in_specs=in_specs, out_specs=out_specs, check_vma=False)
```

```python
import functools

import jax
import jax.numpy as jnp
from jax import lax
from jax.experimental import pallas as pl
from jax.experimental.pallas import tpu as pltpu
from jax.sharding import PartitionSpec as P

SPAN = 4
EPSILON = 1e-06
THETA = 1000000.0
MASKED = -1e30
LOG2E = 1.4426950408889634
NT_DIMS = (((1,), (1,)), ((), ()))
TN_DIMS = (((0,), (0,)), ((), ()))
VMEM_LIMIT = 60 * 1024 * 1024
TILE = 256
CHUNKS = 4
F32 = jnp.float32
LOW = jnp.bfloat16


def rms_scale(values, scales):
    return values * lax.rsqrt(jnp.mean(values * values, axis=-1, keepdims=True) + EPSILON) * scales


def swap(block, axis, mask):
    devices = range(lax.axis_size(axis))
    return lax.ppermute(block, axis, [(i, i ^ mask) for i in devices])


def turn(block, step):
    count = lax.axis_size("ep")
    return lax.ppermute(block, "ep", [(i, (i + 2 * step) % count) for i in range(count)])


def add_low(kept, received):
    return (kept.astype(F32) + received.astype(F32)).astype(LOW)


def halves(block):
    size = block.shape[0] // 2
    return block[:size], block[size:]


def spread_start(slots):
    half = slots[0].shape[0] // 2
    first = jnp.concatenate([rows[:half] for rows in slots], axis=0)
    second = jnp.concatenate([rows[half:] for rows in slots], axis=0)
    sends = [(first, "tp", 2), (second, "ep", 1)]
    return sends, lambda a, b: (jnp.concatenate([first, a]), jnp.concatenate([second, b]))


def spread_next(pair):
    first, second = pair
    sends = [(first, "ep", 1), (second, "tp", 2)]
    return sends, lambda a, b: jnp.concatenate([first, a, second, b])


def spread_last(own):
    return [(own, "tp", 1)], lambda a: a


def collect_start(kept, sent):
    return [(sent, "tp", 1)], lambda a: halves(add_low(kept, a))


def collect_both(pair, first_link, second_link):
    (first, first_sent), (second, second_sent) = halves(pair[0]), halves(pair[1])
    sends = [(first_sent, *first_link), (second_sent, *second_link)]
    return sends, lambda a, b: (add_low(first, a), add_low(second, b))


def collect_next(pair):
    return collect_both(pair, ("ep", 1), ("tp", 2))


def collect_last(pair):
    return collect_both(pair, ("tp", 2), ("ep", 1))


def fold_one(block, axis, mask):
    kept, sent = halves(block)
    return [(sent, axis, mask)], lambda a: add_low(kept, a)


def fold_inner(block, axis, mask):
    parts = block.reshape(2, 2, -1, block.shape[1])
    kept, sent = parts[:, 0], parts[:, 1]
    return [(sent, axis, mask)], lambda a: add_low(kept, a).reshape(-1, block.shape[1])


def tie(*values):
    return lax.optimization_barrier(values)


def now(stage):
    return stage[1](*[swap(x, axis, mask) for x, axis, mask in stage[0]])


def step(stages, compute=None, values=()):
    sends = [[send[0] for send in stage[0]] for stage in stages]
    sends, values = lax.optimization_barrier((sends, values))
    received = [
        [swap(x, axis, mask) for x, (_, axis, mask) in zip(blocks, stage[0])]
        for blocks, stage in zip(sends, stages)
    ]
    result = compute(*values) if compute is not None else values
    received, result = lax.optimization_barrier((received, result))
    return [stage[1](*blocks) for stage, blocks in zip(stages, received)], result


def slot_rows(first, second, count):
    parts = [part.reshape(count, -1, part.shape[1]) for part in (first, second)]
    return jnp.concatenate(parts, axis=1)


def pick(array, index, axis=0):
    return lax.dynamic_index_in_dim(array, index, axis, keepdims=False)


def ep_masks():
    return [1 << n for n in range(lax.axis_size("ep").bit_length() - 1)]


def halve_sum(block, mask):
    bit = lax.axis_index("ep") // mask % 2
    parts = block.reshape(2, -1, block.shape[1])
    kept, sent = pick(parts, bit), pick(parts, 1 - bit)
    return [(sent, "ep", mask)], lambda a: add_low(kept, a)


def double(block, mask):
    bit = lax.axis_index("ep") // mask % 2

    def join(other):
        low = jnp.where(bit == 0, block, other)
        high = jnp.where(bit == 0, other, block)
        return jnp.concatenate([low, high], axis=0)

    return [(block, "ep", mask)], join


def sum_axis(values, axis):
    mask = 1
    while mask < lax.axis_size(axis):
        values = values + swap(values, axis, mask)
        mask *= 2
    return values


def sum_tp(values):
    return sum_axis(values, "tp")


def sum_over_ep(values):
    return sum_axis(values, "ep")


def expert_kernel(
    own_ref,
    other_ref,
    cotangent_own_ref,
    cotangent_other_ref,
    router_ref,
    router_t_ref,
    select_ref,
    gate_ref,
    up_ref,
    down_ref,
    *refs,
):
    grad_keep_ref, grad_send_ref, out_keep_ref, out_send_ref = refs[-10:-6]
    rows_ref, cotangents_ref, hidden_ref, d_gate_ref, d_up_ref, dlog_ref = refs[-6:]
    is_own = pl.program_id(0) < pl.num_programs(0) // 2
    rows = jnp.where(is_own, own_ref[...], other_ref[...])
    model_width = rows.shape[1]
    cotangents = jnp.where(is_own, cotangent_own_ref[...], cotangent_other_ref[...])
    cotangents = cotangents.reshape(rows.shape[0], -1)
    chosen = cotangents[:, model_width : model_width + router_ref.shape[1]].astype(F32)
    logits = jnp.dot(rows, router_ref[...], preferred_element_type=F32)
    logits = jnp.where(chosen > 0.5, logits, MASKED)
    probs = jnp.exp(logits - jnp.max(logits, axis=-1, keepdims=True))
    probs = probs / jnp.sum(probs, axis=-1, keepdims=True)
    select = select_ref[...]
    probs_high = probs.astype(LOW)
    probs_rest = (probs - probs_high.astype(F32)).astype(LOW)
    weight = jnp.dot(probs_high, select, preferred_element_type=F32)
    weight += jnp.dot(probs_rest, select, preferred_element_type=F32)
    gate = lax.dot_general(rows, gate_ref[...], NT_DIMS, preferred_element_type=F32)
    up = lax.dot_general(rows, up_ref[...], NT_DIMS, preferred_element_type=F32)
    d_hidden = (
        lax.dot_general(
            cotangents[:, :model_width], down_ref[...], NT_DIMS, preferred_element_type=F32
        )
        * weight
    )
    sig = 1.0 / (1.0 + jnp.exp(-gate))
    silu = gate * sig
    hidden = silu * up
    d_up = (d_hidden * silu).astype(LOW)
    d_gate = (d_hidden * up * sig * (1.0 + gate * (1.0 - sig))).astype(LOW)
    hidden_low = (hidden * weight).astype(LOW)
    dots = lax.dot_general(
        (d_hidden * hidden).astype(LOW), select, NT_DIMS, preferred_element_type=F32
    )
    dlog = (dots - probs * jnp.sum(dots, axis=-1, keepdims=True)).astype(LOW)

    def store(ref, values):
        ref[...] = values.reshape(ref.shape)

    def store_either(keep_ref, send_ref, values):
        @pl.when(is_own)
        def _():
            store(keep_ref, values)

        @pl.when(jnp.logical_not(is_own))
        def _():
            store(send_ref, values)

    store(rows_ref, rows)
    store(cotangents_ref, cotangents[:, :model_width])
    store(hidden_ref, hidden_low)
    store(d_gate_ref, d_gate)
    store(d_up_ref, d_up)
    store(dlog_ref, dlog)
    outs = jnp.dot(hidden_low, down_ref[...], preferred_element_type=F32).astype(LOW)
    store_either(out_keep_ref, out_send_ref, outs)
    grads = jnp.dot(d_gate, gate_ref[...], preferred_element_type=F32)
    grads += jnp.dot(d_up, up_ref[...], preferred_element_type=F32)
    grads += jnp.dot(dlog, router_t_ref[...], preferred_element_type=F32)
    store_either(grad_keep_ref, grad_send_ref, grads.astype(LOW))


def expert_pass(own, other, cotangents, at, chunk, slots_all, fixed, kept):
    count, model_width = own.shape
    groups, _, unit, wide = cotangents[0].shape
    slots = slots_all // CHUNKS
    half = count // TILE
    width = fixed[-1].shape[0]
    experts_all = fixed[0].shape[1]
    block = TILE // (slots * unit)

    def first(i):
        return jnp.minimum(i, half - 1)

    def second(i):
        return jnp.maximum(i - half, 0)

    def every(i):
        return i

    def rows_spec(index):
        return pl.BlockSpec((TILE, model_width), lambda i: (index(i), 0))

    def placed(columns, index, where):
        return pl.BlockSpec((block, slots, unit, columns), lambda i: (index(i), where, 0, 0))

    def whole(array):
        return pl.BlockSpec(array.shape, lambda i: (0, 0), pipeline_mode=pl.Buffered(1))

    columns = (model_width, model_width, width, width, width, experts_all)
    in_specs = [
        rows_spec(first),
        rows_spec(second),
        placed(wide, first, at),
        placed(wide, second, at),
    ] + [whole(array) for array in fixed]
    loose = 4 if slots_all > CHUNKS else 2
    aliases = {len(in_specs) + n: loose + n for n in range(len(kept))}
    part = jax.ShapeDtypeStruct((count, model_width), LOW)
    place = jax.ShapeDtypeStruct((groups, slots_all, unit, model_width), LOW)
    return pl.pallas_call(
        expert_kernel,
        grid=(2 * half,),
        in_specs=in_specs + [pl.BlockSpec(memory_space=pl.ANY)] * len(kept),
        out_specs=[rows_spec(first), rows_spec(second)]
        + (
            [rows_spec(first), rows_spec(second)]
            if loose == 4
            else [placed(model_width, first, chunk), placed(model_width, second, chunk)]
        )
        + [placed(size, every, chunk) for size in columns],
        out_shape=[part, part]
        + ([part, part] if loose == 4 else [place, place])
        + [jax.ShapeDtypeStruct((2 * groups, slots_all, unit, size), LOW) for size in columns],
        input_output_aliases=aliases,
        compiler_params=pltpu.CompilerParams(vmem_limit_bytes=VMEM_LIMIT),
        cost_estimate=pl.CostEstimate(
            flops=24 * count * model_width * width,
            bytes_accessed=20 * count * model_width,
            transcendentals=2 * count * width,
        ),
        name="expert_pass",
    )(own, other, *cotangents, *fixed, *kept)


def turned_halves(values):
    return pltpu.roll(values, values.shape[1] // 2, 1)


def head_rows(lin, gain, cos, sin):
    scale = lax.rsqrt(jnp.mean(lin * lin, axis=-1, keepdims=True) + EPSILON)
    hat = lin * scale
    normed = hat * gain
    return scale, hat, normed * cos + turned_halves(normed) * sin


def allowed_keys(place_ref, block, keys, queries):
    key_pos = place_ref[2 + block] + lax.broadcasted_iota(jnp.int32, (keys, 1), 0)
    key_pos = jnp.where(key_pos < place_ref[1], -1, key_pos)
    query_pos = place_ref[0] + lax.broadcasted_iota(jnp.int32, (1, queries), 1)
    return key_pos <= query_pos


def attend_kernel(
    place_ref, q_ref, gain_ref, cos_ref, sin_ref, k_ref, v_t_ref, o_ref, norm_ref
):
    queries, head_width = q_ref.shape
    _, _, q_rot = head_rows(q_ref[...], gain_ref[...], cos_ref[...], sin_ref[...])
    q_low = q_rot.astype(LOW)
    factor = head_width ** (-0.5) * LOG2E
    total = jnp.zeros((1, queries), F32)
    acc = jnp.zeros((head_width, queries), F32)
    for block in range(SPAN):
        span = pl.ds(block * queries, queries)
        scores = lax.dot_general(k_ref[span, :], q_low, NT_DIMS, preferred_element_type=F32)
        probs = jnp.where(
            allowed_keys(place_ref, block, queries, queries), jnp.exp2(scores * factor), 0.0
        )
        total += jnp.sum(probs, axis=0, keepdims=True)
        acc += jnp.dot(v_t_ref[:, span], probs.astype(LOW), preferred_element_type=F32)
    o_ref[...] = (acc / total).T.astype(LOW)
    norm_ref[0] = 1.0 / total


def attend(place, q_lin, gain, cos, sin, k_all, v_t):
    tokens, columns = q_lin.shape
    head_width = gain.shape[1]
    heads = columns // head_width
    row = pl.BlockSpec((tokens, head_width), lambda h, p: (0, h))

    def whole(array):
        return pl.BlockSpec(array.shape, lambda h, p: (0, 0))

    return pl.pallas_call(
        attend_kernel,
        grid_spec=pltpu.PrefetchScalarGridSpec(
            num_scalar_prefetch=1,
            grid=(heads,),
            in_specs=[row] + [whole(x) for x in (gain, cos, sin, k_all, v_t)],
            out_specs=[row, pl.BlockSpec((1, 1, tokens), lambda h, p: (h, 0, 0))],
        ),
        out_shape=[
            jax.ShapeDtypeStruct((tokens, columns), LOW),
            jax.ShapeDtypeStruct((heads, 1, tokens), F32),
        ],
        compiler_params=pltpu.CompilerParams(vmem_limit_bytes=VMEM_LIMIT),
        cost_estimate=pl.CostEstimate(
            flops=16 * SPAN * tokens * tokens * columns // 8 * 2,
            bytes_accessed=8 * tokens * columns,
            transcendentals=SPAN * tokens * tokens * heads,
        ),
        name="attend",
    )(place, q_lin, gain, cos, sin, k_all, v_t)


def attend_back_kernel(
    place_ref,
    q_ref,
    d_ref,
    gain_ref,
    cos_ref,
    sin_ref,
    k_ref,
    k_t_ref,
    v_ref,
    norm_ref,
    dq_ref,
    dk_ref,
    dv_ref,
    dgain_ref,
):
    queries, head_width = q_ref.shape
    gain = gain_ref[...]
    scale, hat, q_rot = head_rows(q_ref[...], gain, cos_ref[...], sin_ref[...])
    q_low = q_rot.astype(LOW)
    d_low = d_ref[...]
    shrink = head_width ** (-0.5)
    factor = shrink * LOG2E
    inverse = norm_ref[0]
    delta = jnp.zeros((1, queries), F32)
    kept = []

    @pl.when(pl.program_id(0) == 0)
    def _():
        dk_ref[...] = jnp.zeros_like(dk_ref)
        dv_ref[...] = jnp.zeros_like(dv_ref)
        dgain_ref[...] = jnp.zeros_like(dgain_ref)

    for block in range(SPAN):
        span = pl.ds(block * queries, queries)
        scores = lax.dot_general(k_ref[span, :], q_low, NT_DIMS, preferred_element_type=F32)
        probs = jnp.where(
            allowed_keys(place_ref, block, queries, queries),
            jnp.exp2(scores * factor) * inverse,
            0.0,
        )
        d_probs = lax.dot_general(v_ref[span, :], d_low, NT_DIMS, preferred_element_type=F32)
        delta += jnp.sum(probs * d_probs, axis=0, keepdims=True)
        dv_ref[span, :] += jnp.dot(probs.astype(LOW), d_low, preferred_element_type=F32)
        kept.append((probs, d_probs))
    acc = jnp.zeros((head_width, queries), F32)
    for block in range(SPAN):
        span = pl.ds(block * queries, queries)
        probs, d_probs = kept[block]
        d_scores = (probs * (d_probs - delta)).astype(LOW)
        dk_ref[span, :] += jnp.dot(d_scores, q_low, preferred_element_type=F32) * shrink
        acc += jnp.dot(k_t_ref[:, span], d_scores, preferred_element_type=F32)
    d_rot = acc.T * shrink
    d_normed = d_rot * cos_ref[...] + turned_halves(d_rot * sin_ref[...])
    dgain_ref[...] += jnp.sum(d_normed * hat, axis=0, keepdims=True)
    scaled = d_normed * gain
    d_lin = scale * (scaled - hat * jnp.mean(scaled * hat, axis=-1, keepdims=True))
    dq_ref[...] = d_lin.astype(LOW)


def attend_back(place, q_lin, d_attn, gain, cos, sin, k_all, v_all, inverse):
    tokens, columns = q_lin.shape
    head_width = gain.shape[1]
    heads = columns // head_width
    keys = k_all.shape[0]
    row = pl.BlockSpec((tokens, head_width), lambda h, p: (0, h))
    k_t = k_all.T

    def whole(shape):
        return pl.BlockSpec(shape, lambda h, p: (0, 0))

    fixed = (gain, cos, sin, k_all, k_t, v_all)
    return pl.pallas_call(
        attend_back_kernel,
        grid_spec=pltpu.PrefetchScalarGridSpec(
            num_scalar_prefetch=1,
            grid=(heads,),
            in_specs=[row, row]
            + [whole(x.shape) for x in fixed]
            + [pl.BlockSpec((1, 1, tokens), lambda h, p: (h, 0, 0))],
            out_specs=[
                row,
                whole((keys, head_width)),
                whole((keys, head_width)),
                whole((1, head_width)),
            ],
        ),
        out_shape=[
            jax.ShapeDtypeStruct((tokens, columns), LOW),
            jax.ShapeDtypeStruct((keys, head_width), F32),
            jax.ShapeDtypeStruct((keys, head_width), F32),
            jax.ShapeDtypeStruct((1, head_width), F32),
        ],
        compiler_params=pltpu.CompilerParams(vmem_limit_bytes=VMEM_LIMIT),
        cost_estimate=pl.CostEstimate(
            flops=20 * keys * tokens * columns,
            bytes_accessed=8 * tokens * columns,
            transcendentals=keys * tokens * heads,
        ),
        name="attend_back",
    )(place, q_lin, d_attn, *fixed, inverse)


def body(
    block_in,
    input_norm,
    q_weight,
    k_weight,
    v_weight,
    q_gain,
    k_gain,
    o_weight,
    post_norm,
    router,
    expert_gate,
    expert_up,
    expert_down,
    expert_ids,
    prefix_len,
    out_grad,
):
    tokens, model_width = block_in.shape
    head_width = q_gain.shape[0]
    tp_count = lax.axis_size("tp")
    tp_rank = lax.axis_index("tp")
    ep_count = lax.axis_size("ep")
    ep_rank = lax.axis_index("ep")
    share_rows = tokens // tp_count
    dev_slot = ep_rank % SPAN
    prefix = lax.dynamic_index_in_dim(prefix_len, ep_rank // SPAN, keepdims=False)
    core_bit = tp_rank % 2
    x_bit = tp_rank // 2
    row_index = jnp.arange(tokens, dtype=jnp.int32)
    slots_all = ep_count // 2

    def block_place(slot):
        return (slot + SPAN - 1) % SPAN * tokens

    def my_rows(full_rows):
        return lax.dynamic_slice_in_dim(full_rows, tp_rank * share_rows, share_rows, 0)

    def sum_rows(partial_rows):
        parts = partial_rows.reshape(2, 2, share_rows, -1)

        sent = swap(pick(parts, 1 - core_bit, 1).astype(LOW), "tp", 1)
        parts = pick(parts, core_bit, 1) + sent.astype(F32)
        sent = swap(pick(parts, 1 - x_bit, 0).astype(LOW), "tp", 2)
        return pick(parts, x_bit, 0) + sent.astype(F32)

    def join_rows(rows):
        other = swap(rows, "tp", 2)
        pair = jnp.stack([jnp.where(x_bit == 0, rows, other), jnp.where(x_bit == 0, other, rows)])
        other = swap(pair, "tp", 1)
        low = jnp.where(core_bit == 0, pair, other)
        high = jnp.where(core_bit == 0, other, pair)
        return jnp.stack([low, high], axis=1).reshape(tokens, -1)

    experts_all = router.shape[1]
    local_experts = expert_gate.shape[0]
    hidden_width = expert_gate.shape[2]
    expert_index = jnp.arange(experts_all, dtype=jnp.int32)
    width = local_experts * hidden_width

    chosen = jnp.any(my_rows(expert_ids)[:, :, None] == expert_index[None, None, :], axis=1)
    chosen = jnp.pad(chosen.astype(LOW), ((0, 0), (0, -experts_all % 128)))
    wide_rows = jnp.concatenate([my_rows(out_grad), chosen], axis=1)
    per_chunk = slots_all // CHUNKS
    order = [c * per_chunk + at for c in (0, 1, 3, 2) for at in range(per_chunk)]
    unit = share_rows // 2

    def fetch(rows, positions):
        return [
            rows if order[p] == 0 else turn(rows, slots_all - order[p])
            for c in positions
            for p in range(c * per_chunk, (c + 1) * per_chunk)
        ]

    large = slots_all > CHUNKS
    groups = ((0,), (1,), (2,), (3,)) if large else ((0,), (1, 2), (3,))
    wide_first = now(spread_start(fetch(wide_rows, groups[0])))
    wide_near = [fetch(wide_rows, group) for group in groups[1:-1]]

    x_full = block_in.astype(F32)
    attn_low = rms_scale(x_full, input_norm).astype(LOW)
    k_lin = jnp.dot(attn_low, k_weight, preferred_element_type=F32)
    v_low = jnp.dot(attn_low, v_weight, preferred_element_type=F32).astype(LOW)
    half_width = head_width // 2
    exponents = jnp.arange(half_width, dtype=F32) * (-2.0 / head_width)
    positions = block_place(dev_slot) + row_index
    angles = positions.astype(F32)[:, None] * (THETA**exponents)[None, :]
    cos_half, sin_half = jnp.cos(angles), jnp.sin(angles)
    cos = jnp.concatenate([cos_half, cos_half], axis=1)
    sin = jnp.concatenate([-sin_half, sin_half], axis=1)

    def key_path(lin_rows, scales):
        normed = rms_scale(lin_rows, scales)
        lead, tail = normed[:, :half_width], normed[:, half_width:]
        return normed * cos + jnp.concatenate([tail, lead], axis=1) * sin

    k_rot, k_back = jax.vjp(key_path, k_lin, k_gain)
    pair = jnp.concatenate([k_rot.astype(LOW), v_low], axis=1)
    pair, wide_first = tie(pair, wide_first)
    pairs = [pair] + [swap(pair, "ep", d) for d in range(1, SPAN)]
    wide_first = now(spread_next(wide_first))
    q_lin = jnp.dot(attn_low, q_weight, preferred_element_type=F32)
    gate_cat = expert_gate.transpose(0, 2, 1).reshape(width, -1)
    up_cat = expert_up.transpose(0, 2, 1).reshape(width, -1)
    q_lin, wide_first, wide_rows, pairs, wide_near = tie(
        q_lin, wide_first, wide_rows, pairs, wide_near
    )
    wide_far = fetch(wide_rows, groups[-1])
    wide_near = [now(spread_start(group)) for group in wide_near]
    wide_first_other = now(spread_last(wide_first))
    k_all = jnp.concatenate([p[:, :head_width] for p in pairs], axis=0)
    v_all = jnp.concatenate([p[:, head_width:] for p in pairs], axis=0)
    place = jnp.stack(
        [block_place(dev_slot), prefix] + [block_place(dev_slot ^ d) for d in range(SPAN)]
    ).astype(jnp.int32)
    gain_row = q_gain.reshape(1, -1)
    o_low, inverse = attend(place, q_lin, gain_row, cos, sin, k_all, v_all.T)
    o_low, wide_first_other, wide_near = tie(o_low, wide_first_other, wide_near)
    wide_near = [now(spread_next(group)) for group in wide_near]
    head_part = jnp.dot(o_low, o_weight, preferred_element_type=F32)
    x_mid = my_rows(x_full) + sum_rows(head_part)
    ffn_in, post_norm_back = jax.vjp(rms_scale, x_mid, post_norm)
    ffn_low = ffn_in.astype(LOW)
    ffn_low, wide_far = tie(ffn_low, wide_far)

    own_expert = ep_rank * local_experts + jnp.arange(width, dtype=jnp.int32) // hidden_width
    select = (expert_index[:, None] == own_expert[None, :]).astype(LOW)
    down_cat = expert_down.reshape(width, -1)
    fixed = (router, router.T, select, gate_cat, up_cat, down_cat)
    started = {c: now(spread_start(fetch(ffn_low, (c,)))) for c in range(3)}
    owned = {c: now(spread_next(started[c])) for c in range(2)}
    others = {0: now(spread_last(owned[0])), "wide0": wide_first_other}
    owned["wide0"] = wide_first
    for n, group in enumerate(wide_near):
        owned[f"wide{n + 1}"] = group
    ffn_last = fetch(ffn_low, (3,))

    def shaped(*arrays):
        return [x.reshape(8, -1, unit, x.shape[1]) for x in arrays]

    def apply_experts(at, chunk, own, other, wide_own, wide_other, *kept):
        wide = shaped(wide_own, wide_other)
        return expert_pass(own, other, wide, at, chunk, slots_all, fixed, kept)

    def land(total, chunk, pair):
        rows = slot_rows(*pair, per_chunk)
        for at in range(per_chunk):
            h = order[chunk * per_chunk + at]
            total = total + (rows[at] if h == 0 else turn(rows[at], h)).astype(F32)
        return total

    kept = []
    back, forth = {}, {}
    for chunk in range(CHUNKS):
        names, stages = [], []

        def add(store, key, stage):
            names.append((store, key))
            stages.append(stage)

        if chunk + 1 < CHUNKS:
            add(others, chunk + 1, spread_last(owned[chunk + 1]))
        if chunk + 2 < CHUNKS:
            add(owned, chunk + 2, spread_next(started[chunk + 2]))
        if chunk == 0:
            add(started, 3, spread_start(ffn_last))
            add(started, "far", spread_start(wide_far))
        for n, group in enumerate(groups):
            if group == (3,) and chunk == 1:
                add(owned, f"wide{n}", spread_next(started["far"]))
            if chunk == group[0] - 1:
                add(others, f"wide{n}", spread_last(owned[f"wide{n}"]))
        for store in (back, forth) if large else (back,):
            if chunk >= 1:
                add(store, chunk - 1, collect_start(*store[chunk - 1]))
            if chunk >= 2:
                add(store, chunk - 2, collect_next(store[chunk - 2]))
            if chunk >= 3:
                add(store, chunk - 3, collect_last(store[chunk - 3]))
        n, group = next((n, group) for n, group in enumerate(groups) if chunk in group)
        wide = owned[f"wide{n}"], others[f"wide{n}"]
        at = chunk - group[0]
        results, outs = step(
            stages,
            functools.partial(apply_experts, at, chunk),
            (owned[chunk], others[chunk], *wide, *kept),
        )
        for (store, key), value in zip(names, results):
            store[key] = value
        back[chunk] = outs[:2]
        forth[chunk] = outs[2:4]
        kept = outs[4:] if large else outs[2:]
    rows_all, cotangent_rows, hidden_low, d_gate_low, d_up_low, dlog_low = [
        x.reshape(-1, x.shape[-1]) for x in kept[-6:]
    ]
    if large:
        forth[3] = now(collect_start(*forth[3]))
        forth[2], forth[3] = [now(collect_next(forth[c])) for c in (2, 3)]
        for c in (1, 2, 3):
            forth[c] = now(collect_last(forth[c]))
        out_pair = [jnp.concatenate([forth[c][n] for c in range(CHUNKS)]) for n in range(2)]
        out_pair, rows_all, back = tie(out_pair, rows_all, back)
    else:
        out_keep, out_send = [x.reshape(-1, model_width) for x in kept[:2]]

    def over_rows(left, right):
        return jnp.einsum("ta,tb->ab", left, right, preferred_element_type=F32)

    def split_experts(wide_grad):
        return wide_grad.reshape(local_experts, hidden_width, -1).transpose(0, 2, 1)

    d_ffn = land(jnp.zeros_like(x_mid), 0, back[0])
    (back[1], back[2], back[3]), down_grad = step(
        [collect_last(back[1]), collect_next(back[2]), collect_start(*back[3])],
        over_rows,
        (hidden_low, cotangent_rows),
    )
    down_grad = down_grad.reshape(expert_down.shape)
    d_ffn = land(d_ffn, 1, back[1])
    (back[2], back[3]), gate_grad = step(
        [collect_last(back[2]), collect_next(back[3])], over_rows, (d_gate_low, rows_all)
    )
    d_ffn = land(d_ffn, 2, back[2])
    (back[3],), router_grad_t = step([collect_last(back[3])], over_rows, (dlog_low, rows_all))
    d_ffn = land(d_ffn, 3, back[3])

    d_mid_norm, post_norm_grad = post_norm_back(d_ffn)
    d_mid = my_rows(out_grad).astype(F32) + d_mid_norm
    if large:
        d_mid_low = join_rows(d_mid.astype(LOW))
    else:
        (out_pair,), d_mid_low = step(
            [collect_start(out_keep, out_send)], join_rows, (d_mid.astype(LOW),)
        )
    o_sum = jnp.einsum("tj,td->jd", o_low, d_mid_low, preferred_element_type=F32).astype(LOW)
    d_attn_low = jnp.einsum(
        "td,jd->tj", d_mid_low, o_weight, preferred_element_type=F32
    ).astype(LOW)
    masks = ep_masks()
    out_first, out_second = out_pair
    d_attn_low, o_sum, out_first, out_second = tie(d_attn_low, o_sum, out_first, out_second)
    o_sum = now(halve_sum(o_sum, masks[0]))
    if not large:
        out_second = now(fold_one(out_second, "tp", 2))
    dq_low, dk_all, dv_all, q_gain_grad = attend_back(
        place, q_lin, d_attn_low, gain_row, cos, sin, k_all, v_all, inverse
    )
    dq_low, dk_all, dv_all, o_sum, out_first, out_second = tie(
        dq_low, dk_all, dv_all, o_sum, out_first, out_second
    )
    if not large:
        out_first = now(fold_inner(out_first, "tp", 2))
    for mask in masks[1:]:
        o_sum = now(halve_sum(o_sum, mask))
    split = dq_low.shape[1] // 2
    first_sum = jnp.einsum(
        "td,tj->dj", attn_low, dq_low[:, :split], preferred_element_type=F32
    ).astype(LOW)
    first_sum = now(halve_sum(first_sum, masks[0]))
    pair_grad = jnp.concatenate([dk_all, dv_all], axis=1)
    total = pair_grad[:tokens]
    for d in range(1, SPAN):
        part = pair_grad[d * tokens : (d + 1) * tokens].astype(LOW)
        total = total + swap(part, "ep", d).astype(F32)
    dk_lin, k_gain_grad = k_back(total[:, :head_width])
    dk_low = dk_lin.astype(LOW)
    dv_low = total[:, head_width:].astype(LOW)
    second_sum = jnp.einsum(
        "td,tj->dj",
        attn_low,
        jnp.concatenate([dq_low[:, split:], dk_low, dv_low], axis=1),
        preferred_element_type=F32,
    ).astype(LOW)
    d_attn_in = jnp.einsum("tj,dj->td", dq_low, q_weight, preferred_element_type=F32)
    d_attn_in = d_attn_in + jnp.einsum("tj,dj->td", dk_low, k_weight, preferred_element_type=F32)
    d_attn_in = d_attn_in + jnp.einsum("tj,dj->td", dv_low, v_weight, preferred_element_type=F32)

    second_sum = now(halve_sum(second_sum, masks[0]))
    for mask in masks[1:]:
        first_sum = now(halve_sum(first_sum, mask))
    for mask in masks[:0:-1]:
        o_sum = now(double(o_sum, mask))
    d_attn_rows = sum_rows(d_attn_in)
    _, input_norm_back = jax.vjp(rms_scale, my_rows(x_full), input_norm)
    d_in_norm, input_norm_grad = input_norm_back(d_attn_rows)
    input_rows = (d_mid + d_in_norm).astype(LOW)
    gains = jnp.concatenate([q_gain_grad.reshape(-1), k_gain_grad])
    small = jnp.concatenate(
        [
            router_grad_t,
            post_norm_grad[None],
            input_norm_grad[None],
            jnp.pad(gains, (0, model_width - gains.shape[0]))[None],
        ],
        axis=0,
    )
    first_sum, second_sum, o_sum, small, input_rows, out_first, out_second, gate_grad = tie(
        first_sum, second_sum, o_sum, small, input_rows, out_first, out_second, gate_grad
    )
    o_sum = now(double(o_sum, masks[0]))
    for mask in masks[1:]:
        second_sum = now(halve_sum(second_sum, mask))
    for mask in masks[:0:-1]:
        first_sum = now(double(first_sum, mask))
    up_grad = over_rows(d_up_low, rows_all)
    small = sum_tp(small)
    input_grad = join_rows(input_rows)
    first_sum, second_sum, o_sum, small, up_grad, out_first, out_second = tie(
        first_sum, second_sum, o_sum, small, up_grad, out_first, out_second
    )
    first_sum = now(double(first_sum, masks[0]))
    for mask in masks[:0:-1]:
        second_sum = now(double(second_sum, mask))
    if not large:
        out_first = now(fold_one(out_first, "ep", 1))
        out_second = now(fold_one(out_second, "ep", 1))
    first_sum, second_sum, small, out_first, out_second, gate_grad, up_grad = tie(
        first_sum, second_sum, small, out_first, out_second, gate_grad, up_grad
    )
    second_sum = now(double(second_sum, masks[0]))
    small = sum_over_ep(small)
    gate_grad, up_grad = split_experts(gate_grad), split_experts(up_grad)
    out_slots = slot_rows(out_first, out_second, slots_all)
    mixed = out_slots[0].astype(F32)
    for p in range(1, slots_all):
        mixed = mixed + turn(out_slots[p], order[p]).astype(F32)
    block_rows = (x_mid + mixed).astype(LOW)
    block_out = lax.all_to_all(block_rows, "tp", split_axis=1, concat_axis=0, tiled=True)
    o_weight_grad = o_sum.astype(F32)
    q_weight_grad = jnp.concatenate([first_sum, second_sum[:, :split]], axis=1).astype(F32)
    k_weight_grad = second_sum[:, split : split + head_width].astype(F32)
    v_weight_grad = second_sum[:, split + head_width :].astype(F32)
    router_grad = small[:experts_all].T
    post_norm_grad, input_norm_grad, gains = small[experts_all : experts_all + 3]
    return (
        block_out,
        input_grad,
        input_norm_grad,
        q_weight_grad,
        k_weight_grad,
        v_weight_grad,
        gains[:head_width],
        gains[head_width : 2 * head_width],
        o_weight_grad,
        post_norm_grad,
        router_grad,
        gate_grad,
        up_grad,
        down_grad,
    )


def solution(mesh):
    in_specs = (
        P("ep", None),
        P(),
        P(None, "tp"),
        P(None, "tp"),
        P(None, "tp"),
        P(),
        P(),
        P("tp", None),
        P(),
        P(),
        P("ep", None, "tp"),
        P("ep", None, "tp"),
        P("ep", "tp", None),
        P("ep", None),
        P(),
        P("ep", None),
    )
    out_specs = (
        P("ep", "tp"),
        P("ep", None),
        P(),
        P(None, "tp"),
        P(None, "tp"),
        P(None, "tp"),
        P(),
        P(),
        P("tp", None),
        P(),
        P(),
        P("ep", None, "tp"),
        P("ep", None, "tp"),
        P("ep", "tp", None),
    )
    return jax.shard_map(body, mesh=mesh, in_specs=in_specs, out_specs=out_specs, check_vma=False)
```
